128 devices in a mesh: mem: 8 (over z_lo, y), tile: 16 (over x, z_hi, core).
Axes of the slice: x: 4, y: 4, z: 4 (z_hi: 2, z_lo: 2; z = z_hi * 2 + z_lo), core: 2. Of those that a mesh axis runs over, the one named last changes fastest.
Arguments:
- hidden_in: bfloat16 [32, 4096, 1024], P('mem', 'tile'), may hold values from -6 to 6
- norm_gain: bfloat16 [1024], replicated, may hold values from 0.5 to 1.5
- w_in: bfloat16 [1024, 4096], replicated, may hold values from -0.1875 to 0.1875
- w_out: bfloat16 [4096, 1024], replicated, may hold values from -0.09375 to 0.09375
- w_dec: bfloat16 [69, 1024], replicated, may hold values from -0.1875 to 0.1875
- observed: float32 [69, 256, 16], P(None, 'tile'), may hold values from -16 to 16
- obs_count: int32 [69, 256, 16], P(None, 'tile'), may hold values from 0 to 3, as said below
- obs_error: float32 [69], replicated, may hold values from 2 to 6
Outputs:
- increments: float32 [32, 69, 16, 256], P('mem', None, 'tile')
The draws below stay inside these ranges and needn't reach their ends.
Inputs may be any that keep to these rules, and one draw needn't show every extreme that they name: `obs_count`: each entry is 0 or 3 and is the same for all variables at a grid point; it is 3 exactly where one of 5 observed latitude rows meets one of 192 observed longitude columns.
All inputs are finite; a program needn't handle non-finite values.
Results may differ from the reference program's by a relative error of at most 0.02.
Values may be sent and summed in bfloat16 or wider, within the bound.
No kernel may reach another device: no remote copies, remote signals or barrier semaphores. Data moves between devices by JAX's collectives and lax.ppermute only.
A program may use at most 128 MiB of HBM per device.

```python
import math
import jax
import jax.numpy as jnp
from jax import lax

D = 1024
FF = 4096
VARS = 69
RAD = 6
NS_ITERS = 4
MEMBERS = 32
LAT = 16
LON = 256
TOKENS = 4096


def smooth_loadings(loading_key, reach):
    single = jax.random.normal(loading_key, (MEMBERS, LAT, LON, 2), jnp.float32)
    summed = single
    for offset in range(1, reach):
        summed = summed + jnp.roll(single, offset, axis=2)
    return (summed / math.sqrt(reach)).reshape(MEMBERS, TOKENS, 2)


def draw_hidden_in(key, part):
    key = jax.random.fold_in(key, 11)
    perturbation_key, loading_key, pattern_key = jax.random.split(key, 3)
    reach = 4
    common_gain = 0.5
    noise_gain = 0.6
    member_noise = jax.random.normal(perturbation_key, (MEMBERS, TOKENS, D), jnp.float32)
    loadings = smooth_loadings(loading_key, reach)
    patterns = jax.random.normal(pattern_key, (3, TOKENS, D), jnp.float32)
    common = loadings[:, :, 0:1] * patterns[0][None] + loadings[:, :, 1:2] * patterns[1][None]
    state = 0.6 * patterns[2][None] + common_gain * common + noise_gain * member_noise
    return jnp.clip(state, -6.0, 6.0).astype(jnp.bfloat16)


def draw_obs_count(key, part):
    key = jax.random.fold_in(key, 23)
    row_key, column_key = jax.random.split(key, 2)
    row_rank = jax.random.permutation(row_key, LAT)
    column_rank = jax.random.permutation(column_key, LON)
    row_on = (row_rank < max(1, LAT // 3)).astype(jnp.int32)
    column_on = (column_rank < LON - LON // 4).astype(jnp.int32)
    grid_count = 3 * column_on[:, None] * row_on[None, :]
    return jnp.broadcast_to(grid_count[None, :, :], (VARS, LON, LAT)).astype(jnp.int32)


def steps_of(rng, extent, cuts, smallest, high):
    gain = 1.0
    for position, shards_of in cuts:
        heights = jax.random.uniform(jax.random.fold_in(jax.random.fold_in(rng, 6), position), (shards_of,), jnp.float32, smallest / len(cuts), high / len(cuts))
        gain = gain * jnp.repeat(jnp.exp(heights), extent[position] // shards_of).reshape((-1,) + (1,) * (len(extent) - 1 - position))
    return gain


def scatter_about(own_key, extent, scale, most, cuts=(), held_as=jnp.bfloat16):
    result = scale * jax.random.normal(own_key, extent, jnp.float32)
    if cuts:
        result = result * steps_of(own_key, extent, cuts, -0.22, 0.18)
    return jnp.clip(result, -most, most).astype(held_as)


def setup_inputs(seed: int = 0) -> dict:
    streams_of = jax.random.split(jax.random.key(seed), 9)
    hidden_in = draw_hidden_in(jax.random.fold_in(streams_of[8], 71), 0)
    norm_gain = jnp.clip(1.0 + 0.1 * jax.random.normal(streams_of[1], (D,), jnp.float32), 0.5, 1.5).astype(jnp.bfloat16)
    w_in = scatter_about(streams_of[2], (D, FF), D ** -0.5, 0.1875)
    w_out = scatter_about(streams_of[3], (FF, D), FF ** -0.5, 0.09375)
    w_dec = scatter_about(streams_of[4], (VARS, D), D ** -0.5, 0.1875)
    observed = scatter_about(streams_of[5], (VARS, LON, LAT), 4.0, 16.0, ((1, 16),), jnp.float32)
    obs_count = draw_obs_count(jax.random.fold_in(streams_of[8], 71), 0)
    obs_error = jnp.clip(jnp.exp(jax.random.uniform(streams_of[7], (VARS,), jnp.float32, math.log(2.0), math.log(6.0))), 2.0, 6.0)
    return {"hidden_in": hidden_in, "norm_gain": norm_gain, "w_in": w_in, "w_out": w_out, "w_dec": w_dec, "observed": observed, "obs_count": obs_count, "obs_error": obs_error}


precision_level = lax.Precision.HIGHEST

def taper_weights(offsets):
    ratio = offsets.astype(jnp.float32) / (RAD + 1.0)
    return jnp.where(jnp.abs(offsets) <= RAD, (1.0 - ratio * ratio) ** 2, 0.0).astype(jnp.float32)

def transform(gram, innov_vec):
    count = gram.shape[0]
    unit = jnp.eye(count, dtype=jnp.float32)[:, :, None]
    frob_norm = jnp.sqrt(lax.optimization_barrier(jnp.sum(gram * gram, axis=(0, 1))))
    root_iter = gram / frob_norm
    inv_root = jnp.broadcast_to(unit, gram.shape)
    for sweep in range(NS_ITERS):
        correction = 1.5 * unit - 0.5 * jnp.einsum('ijb,jkb->ikb', inv_root, root_iter, precision=precision_level)
        root_iter = jnp.einsum('ijb,jkb->ikb', root_iter, correction, precision=precision_level)
        inv_root = jnp.einsum('ijb,jkb->ikb', correction, inv_root, precision=precision_level)
    inverse = jnp.einsum('ijb,jkb->ikb', inv_root, inv_root, precision=precision_level) / frob_norm
    mean_weights = jnp.einsum('ikb,kb->ib', inverse, innov_vec, precision=precision_level)
    return (math.sqrt(count - 1.0) * inv_root / jnp.sqrt(frob_norm) + mean_weights[:, None, :]).astype(jnp.bfloat16)

def reference(hidden_in, norm_gain, w_in, w_out, w_dec, observed, obs_count, obs_error):

    def member_fields(tokens):
        xf = tokens.astype(jnp.float32)
        centre = lax.optimization_barrier(jnp.mean(xf, axis=-1, keepdims=True))
        spread = lax.optimization_barrier(jnp.mean((xf - centre) ** 2, axis=-1, keepdims=True))
        normed = ((xf - centre) * lax.rsqrt(spread + 1e-05) * norm_gain.astype(jnp.float32)).astype(jnp.bfloat16)
        act = jax.nn.gelu(jnp.dot(normed, w_in, preferred_element_type=jnp.float32)).astype(jnp.bfloat16)
        layer_out = (xf + jnp.dot(act, w_out, preferred_element_type=jnp.float32)).astype(jnp.bfloat16)
        return jnp.dot(w_dec, layer_out.T, preferred_element_type=jnp.float32)
    fields = lax.map(member_fields, hidden_in).reshape(MEMBERS, VARS, LAT, LON)
    mean = lax.optimization_barrier(jnp.sum(fields, axis=0)) / MEMBERS
    anomaly = fields - mean
    anom_b = anomaly.astype(jnp.bfloat16)
    prec = obs_count.transpose(0, 2, 1).astype(jnp.float32) / (obs_error ** 2)[:, None, None]
    weight_applied = (anomaly * prec).astype(jnp.bfloat16)
    observation_departure = observed.transpose(0, 2, 1) - mean
    pairs = jnp.einsum('ivab,kvab->ikab', weight_applied.astype(jnp.float32), anom_b.astype(jnp.float32), precision=precision_level)
    departure_rows = jnp.einsum('wjmz,jmz->wmz', weight_applied.astype(jnp.float32), observation_departure, precision=precision_level)
    stacked = jnp.concatenate([pairs, departure_rows[:, None]], axis=1)
    spread_lon = jnp.zeros_like(stacked)
    for offset in range(-RAD, RAD + 1):
        spread_lon = spread_lon + taper_weights(jnp.array(offset, dtype=jnp.int32)) * jnp.roll(stacked, -offset, axis=3)
    lat_ids = jnp.arange(LAT, dtype=jnp.int32)
    lat_taper = taper_weights(lat_ids[:, None] - lat_ids[None, :])
    local = jnp.einsum('ab,ikbj->ikaj', lat_taper, spread_lon, precision=precision_level)
    gram = local[:, :MEMBERS] + (MEMBERS - 1.0) * jnp.eye(MEMBERS, dtype=jnp.float32)[:, :, None, None]
    coeffs = transform(gram.reshape(MEMBERS, MEMBERS, LAT * LON), local[:, MEMBERS].reshape(MEMBERS, LAT * LON))
    mixed = jnp.einsum('kvp,kmp->mvp', anom_b.astype(jnp.float32).reshape(MEMBERS, VARS, LAT * LON), coeffs.astype(jnp.float32), precision=precision_level)
    return (mixed - anomaly.reshape(MEMBERS, VARS, LAT * LON)).reshape(MEMBERS, VARS, LAT, LON)
```

```python
import functools
import math

import jax
import jax.numpy as jnp
import numpy as np
from jax import lax
from jax.experimental import pallas as pl
from jax.experimental.pallas import tpu as pltpu
from jax.sharding import PartitionSpec as P

RAD = 6
NS_ITERS = 4
F32 = jnp.float32
BF16 = jnp.bfloat16

LANES = 128
VROWS = 72
HROWS = 40
HALO = 8
SECTOR = 32
MEMBERS = 32
GROUP = 4
DIAGS = MEMBERS // 2 + 1
ROWS = DIAGS + 1
FF_BLOCK = 1024
TOKEN_BLOCK = 512

VMEM = pltpu.CompilerParams(vmem_limit_bytes=60 * 2**20)


def lanes_of(shape):
    return lax.broadcasted_iota(jnp.int32, shape, len(shape) - 1)


def gelu(h):
    inner = h * (math.sqrt(2.0 / math.pi) + (0.044715 * math.sqrt(2.0 / math.pi)) * (h * h))
    half = 0.5 * h
    return half + half * jnp.tanh(inner)


def forecast_kernel(x_ref, gain_ref, win_ref, wout_ref, wdec_ref, out_ref, normed, acc):
    step = pl.program_id(0)
    steps = pl.num_programs(0)
    tokens = x_ref.shape[0]
    blocks = tokens // TOKEN_BLOCK
    lon_all = tokens // GROUP

    @pl.when(step == 0)
    def _():
        gain = gain_ref[...].astype(F32)
        for r in range(tokens // 128):
            xf = x_ref[pl.ds(r * 128, 128), :].astype(F32)
            centred = xf - jnp.mean(xf, axis=-1, keepdims=True)
            spread = jnp.mean(centred * centred, axis=-1, keepdims=True)
            normed[pl.ds(r * 128, 128), :] = (centred * lax.rsqrt(spread + 1e-05) * gain).astype(BF16)

    def up(r):
        return jnp.dot(
            normed[pl.ds(r * TOKEN_BLOCK, TOKEN_BLOCK), :], win_ref[...], preferred_element_type=F32
        )

    def run(first):
        hidden = up(0)
        for r in range(blocks):
            following = up(r + 1) if r + 1 < blocks else None
            down = jnp.dot(gelu(hidden).astype(BF16), wout_ref[...], preferred_element_type=F32)
            at = pl.ds(r * TOKEN_BLOCK, TOKEN_BLOCK)
            if first:
                acc[at, :] = down
            else:
                acc[at, :] += down
            hidden = following

    @pl.when(step == 0)
    def _():
        run(True)

    @pl.when(step > 0)
    def _():
        run(False)

    @pl.when(step == steps - 1)
    def _():
        acc[...] = x_ref[...].astype(F32) + acc[...]
        wdec = wdec_ref[...]
        contract = (((1,), (1,)), ((), ()))
        for i in range(lon_all // SECTOR):
            main, halo = [], []
            for m in range(GROUP):
                base = m * lon_all
                main.append(acc[pl.ds(base + SECTOR * i, SECTOR), :])
                halo.append(acc[pl.ds(base + (SECTOR * i - HALO) % lon_all, HALO), :])
                halo.append(acc[pl.ds(base + (SECTOR * (i + 1)) % lon_all, HALO), :])
            main = jnp.concatenate(main, axis=0).astype(BF16)
            halo = jnp.concatenate(halo, axis=0).astype(BF16)
            main = lax.dot_general(wdec, main, contract, preferred_element_type=F32)
            halo = lax.dot_general(wdec, halo, contract, preferred_element_type=F32)
            halo = jnp.concatenate([halo[:HROWS], halo[HROWS:]], axis=1)
            out_ref[i] = jnp.concatenate([main[:VROWS], halo], axis=0).astype(BF16)


def forecast(x, gain, w_in, w_out, w_dec):
    tokens, width = x.shape
    hidden = w_in.shape[1]
    sectors = tokens // GROUP // SECTOR
    return pl.pallas_call(
        forecast_kernel,
        grid=(hidden // FF_BLOCK,),
        in_specs=[
            pl.BlockSpec((tokens, width), lambda s: (0, 0)),
            pl.BlockSpec((1, width), lambda s: (0, 0)),
            pl.BlockSpec((width, FF_BLOCK), lambda s: (0, s)),
            pl.BlockSpec((FF_BLOCK, width), lambda s: (s, 0)),
            pl.BlockSpec((2 * HROWS, width), lambda s: (0, 0)),
        ],
        out_specs=pl.BlockSpec((sectors, VROWS + HROWS, LANES), lambda s: (0, 0, 0)),
        out_shape=jax.ShapeDtypeStruct((sectors, VROWS + HROWS, LANES), BF16),
        scratch_shapes=[pltpu.VMEM((tokens, width), BF16), pltpu.VMEM((tokens, width), F32)],
        compiler_params=VMEM,
        cost_estimate=pl.CostEstimate(
            flops=4 * tokens * width * hidden, bytes_accessed=4 * width * hidden, transcendentals=0
        ),
        name="forecast",
    )(x, gain, w_in, w_out, w_dec)


def copies_over_lanes(tile, width):
    while width < LANES:
        tile = tile + pltpu.roll(tile, width, 1)
        width *= 2
    return tile


def sum_over_groups(tile, width):
    while width < LANES:
        tile = tile + pltpu.roll(tile, width, 1)
        width *= 2
    return tile


def shifted_tile(tiles, index, shift, width):
    move = shift * width
    if not move:
        return tiles(index)
    here = pltpu.roll(tiles(index), LANES - move, 1)
    there = pltpu.roll(tiles(index + 1), LANES - move, 1)
    return jnp.where(lanes_of(here.shape) < LANES - move, here, there)


def pair_sums(fields, observed, inv_count, width, weighted, moved, anomalies, put):
    count = len(fields)
    per = LANES // width
    total = fields[0]
    for tile in fields[1:]:
        total = total + tile
    mean = sum_over_groups(total, width) / MEMBERS
    for k in range(count):
        anomaly = fields[k] - mean
        if anomalies is not None:
            anomalies[k] = anomaly
        weighted[k] = (anomaly * inv_count).astype(BF16).astype(F32)
        moved[0, k] = anomaly.astype(BF16).astype(F32)
    for t in range(1, per):
        for k in range(count):
            moved[t, k] = shifted_tile(lambda j: moved[0, j % count], k, t, width)
    innovation = observed - mean
    for k in range(count):
        put(DIAGS, k, jnp.sum(weighted[k] * innovation, axis=0, keepdims=True))
    for s in range(DIAGS):
        on, t = divmod(s, per)
        for k in range(count):
            put(s, k, jnp.sum(weighted[k] * moved[t, (k + on) % count], axis=0, keepdims=True))


def pairs_kernel(
    place_ref, recv_ref, obs_ref, err_ref, taper_ref, out_ref, anom_ref,
    weighted, moved, weighted_halo, moved_halo, sums,
):
    tiles = recv_ref.shape[0]
    lon_all = obs_ref.shape[1]
    obs = pltpu.roll(obs_ref[...], lax.rem(lon_all - SECTOR * place_ref[0], lon_all), 1)
    first, last = obs[:, :LANES], obs[:, lon_all - LANES :]
    lane = lanes_of(first.shape)
    obs_main = copies_over_lanes(jnp.where(lane < SECTOR, first, 0.0), SECTOR)
    obs_halo = jnp.where(
        lane < HALO,
        pltpu.roll(last, HALO, 1),
        jnp.where(lane < 2 * HALO, pltpu.roll(first, LANES - SECTOR + HALO, 1), 0.0),
    )
    obs_halo = copies_over_lanes(obs_halo, 2 * HALO)
    variables = VROWS - 3
    err = err_ref[...]
    prec_main = obs_main[variables : variables + 1] / (err * err)
    prec_halo = obs_halo[variables : variables + 1] / (err * err)

    sums[...] = jnp.zeros_like(sums)

    def put_main(s, k, row):
        sums[pl.ds(s * tiles + k, 1), 0:LANES] = row

    def put_halo(s, k, row):
        sums[pl.ds(s * tiles + 2 * k, 1), LANES : 2 * LANES] = row
        sums[pl.ds(s * tiles + 2 * k + 1, 1), 2 * LANES : 3 * LANES] = row

    fields, halos = [], []
    for m in range(tiles):
        both = recv_ref[m].astype(F32)
        fields.append(both[:VROWS])
        halos.append(both[VROWS:])
    left = lanes_of((HROWS, LANES)) < LANES // 2
    halo_fields = []
    for h in range(tiles // 2):
        a, b = halos[2 * h], halos[2 * h + 1]
        upper = jnp.where(left, a, pltpu.roll(b, LANES // 2, 1))
        lower = jnp.where(left, pltpu.roll(a, LANES // 2, 1), b)
        halo_fields.append(jnp.concatenate([upper, lower], axis=0)[:VROWS])
    pair_sums(fields, obs_main, prec_main, SECTOR, weighted, moved, anom_ref, put_main)
    pair_sums(halo_fields, obs_halo, prec_halo, 2 * HALO, weighted_halo, moved_halo, None, put_halo)
    smooth = jnp.dot(
        sums[...], taper_ref[...], precision=lax.Precision.HIGHEST, preferred_element_type=F32
    ).astype(BF16)
    for a in range(out_ref.shape[0]):
        out_ref[a] = smooth


def taper_of(offset):
    offset = np.asarray(offset, np.float32)
    ratio = offset / np.float32(RAD + 1.0)
    return np.where(np.abs(offset) <= RAD, (1.0 - ratio * ratio) ** 2, 0.0).astype(np.float32)


def longitude_taper():
    out_member, out_col = np.divmod(np.arange(LANES), SECTOR)
    main_member, main_col = np.divmod(np.arange(LANES), SECTOR)
    halo_member, halo_place = np.divmod(np.arange(LANES), 2 * HALO)
    halo_col = np.where(halo_place < HALO, halo_place - HALO, halo_place - HALO + SECTOR)
    parts = []
    for member, col in (
        (main_member, main_col), (halo_member, halo_col), (halo_member - GROUP, halo_col)
    ):
        same = member[:, None] == out_member[None, :]
        parts.append(np.where(same, taper_of(col[:, None] - out_col[None, :]), 0.0))
    return jnp.asarray(np.concatenate(parts, axis=0).astype(np.float32))


def pairs(place, recv, obs, err, n_rows):
    tiles = recv.shape[0]
    full = pl.BlockSpec(memory_space=pltpu.VMEM)
    return pl.pallas_call(
        pairs_kernel,
        in_specs=[pl.BlockSpec(memory_space=pltpu.SMEM), full, full, full, full],
        out_specs=(full, full),
        out_shape=(
            jax.ShapeDtypeStruct((n_rows, ROWS * tiles, LANES), BF16),
            jax.ShapeDtypeStruct((tiles, VROWS, LANES), F32),
        ),
        scratch_shapes=[
            pltpu.VMEM((tiles, VROWS, LANES), F32),
            pltpu.VMEM((LANES // SECTOR, tiles, VROWS, LANES), F32),
            pltpu.VMEM((tiles // 2, VROWS, LANES), F32),
            pltpu.VMEM((LANES // (2 * HALO), tiles // 2, VROWS, LANES), F32),
            pltpu.VMEM((ROWS * tiles, 3 * LANES), F32),
        ],
        compiler_params=VMEM,
        name="pairs",
    )(place, recv, obs, err, longitude_taper())


def on_by(x, n):
    sub, t = divmod(n % MEMBERS, GROUP)
    if t:
        move = LANES - SECTOR * t
        x = pltpu.roll(x, move, 1)
        x = jnp.where(lanes_of(x.shape) < move, x, pltpu.roll(x, 7, 0))
    if sub:
        x = pltpu.roll(x, 8 - sub, 0)
    return x


def shifted_sum(term):
    total = None
    for t in range(GROUP - 1, -1, -1):
        inner = None
        for a in range(MEMBERS // GROUP - 1, -1, -1):
            part = term(GROUP * a + t)
            inner = part if inner is None else on_by(inner, GROUP) + part
        total = inner if total is None else on_by(total, 1) + inner
    return total


def product(left, right, out, scale=None, shift=None):
    for s in range(DIAGS):
        value = shifted_sum(lambda t: left[(-t) % MEMBERS] * right[(s - t) % MEMBERS])
        if scale is not None:
            value = scale * value
            if s == 0:
                value = value + shift
        out[s] = value
    mirror(out)


def mirror(out):
    for s in range(1, MEMBERS - DIAGS + 1):
        out[MEMBERS - s] = on_by(out[s], -s)


def transform_kernel(lat_ref, recv_ref, anom_ref, out_ref, bank, moved, coeff):
    rows = recv_ref.shape[0]
    tiles = anom_ref.shape[0]
    local = lat_ref[0] * recv_ref[0].astype(F32)
    for b in range(1, rows):
        local = local + lat_ref[b] * recv_ref[b].astype(F32)
    diag = [local[s * tiles : (s + 1) * tiles] for s in range(ROWS)]
    innov = diag[DIAGS]
    diag[0] = diag[0] + (MEMBERS - 1.0)
    gram, root, inv_root, corr = bank.at[0], bank.at[1], bank.at[2], bank.at[3]
    other_root, other_inv = bank.at[4], bank.at[5]
    square = None
    for s in range(DIAGS):
        part = diag[s] * diag[s]
        if 0 < s < DIAGS - 1:
            part = part + part
        square = part if square is None else square + part
    square = jnp.broadcast_to(jnp.sum(square, axis=0, keepdims=True), square.shape)
    frob = jnp.sqrt(sum_over_groups(square, SECTOR))
    inv_frob = 1.0 / frob
    for s in range(DIAGS):
        gram[s] = diag[s] * inv_frob
    mirror(gram)
    for s in range(MEMBERS):
        inv_root[s] = -0.5 * gram[s] + (1.5 if s == 0 else 0.0)
    product(gram, inv_root, root)
    for sweep in range(1, NS_ITERS):
        product(inv_root, root, corr, -0.5, 1.5)
        if sweep < NS_ITERS - 1:
            product(root, corr, other_root)
        product(corr, inv_root, other_inv)
        root, other_root = other_root, root
        inv_root, other_inv = other_inv, inv_root
    half = shifted_sum(lambda t: inv_root[(-t) % MEMBERS] * innov)
    mean_weights = shifted_sum(lambda t: inv_root[(-t) % MEMBERS] * half) * inv_frob
    factor = math.sqrt(MEMBERS - 1.0) / jnp.sqrt(frob)
    for s in range(MEMBERS):
        value = inv_root[s] * factor + on_by(mean_weights, s)
        coeff[pl.ds(s * tiles, tiles), :] = value.astype(BF16).astype(F32)
    for k in range(tiles):
        moved[0, k] = anom_ref[k].astype(BF16).astype(F32)
    for t in range(1, GROUP):
        for k in range(tiles):
            moved[t, k] = shifted_tile(lambda j: moved[0, j % tiles], k, t, SECTOR)
    for k in range(tiles):
        mixed = None
        for s in range(MEMBERS):
            on, t = divmod(s, GROUP)
            part = moved[t, (k + on) % tiles] * coeff[pl.ds(s * tiles + k, 1), :]
            mixed = part if mixed is None else mixed + part
        out_ref[k] = (mixed - anom_ref[k]).astype(BF16)


def transform(lat_taper, recv, anomaly):
    tiles = anomaly.shape[0]
    full = pl.BlockSpec(memory_space=pltpu.VMEM)
    return pl.pallas_call(
        transform_kernel,
        in_specs=[pl.BlockSpec(memory_space=pltpu.SMEM), full, full],
        out_specs=full,
        out_shape=jax.ShapeDtypeStruct((tiles, VROWS, LANES), BF16),
        scratch_shapes=[
            pltpu.VMEM((6, MEMBERS, tiles, LANES), F32),
            pltpu.VMEM((GROUP, tiles, VROWS, LANES), F32),
            pltpu.VMEM((MEMBERS * tiles, LANES), F32),
        ],
        compiler_params=VMEM,
        name="transform",
    )(lat_taper, recv, anomaly)


def strips_kernel(recv_ref, out_ref):
    tiles = recv_ref.shape[0]
    variables = out_ref.shape[1]
    parts = [recv_ref[i].astype(F32) for i in range(tiles)]
    group = lanes_of(parts[0].shape) // SECTOR
    for m in range(GROUP):
        for c in range(tiles // GROUP):
            tile = None
            for j in range(GROUP):
                piece = parts[GROUP * c + j]
                if j != m:
                    piece = pltpu.roll(piece, (SECTOR * (j - m)) % LANES, 1)
                tile = piece if tile is None else jnp.where(group == j, piece, tile)
            out_ref[m, :, pl.ds(c * LANES, LANES)] = tile[:variables]


def strips(recv, variables):
    tiles = recv.shape[0]
    full = pl.BlockSpec(memory_space=pltpu.VMEM)
    return pl.pallas_call(
        strips_kernel,
        in_specs=[full],
        out_specs=full,
        out_shape=jax.ShapeDtypeStruct((GROUP, variables, tiles * SECTOR), F32),
        compiler_params=VMEM,
        name="strips",
    )(recv)


def body(hidden_in, norm_gain, w_in, w_out, w_dec, observed, obs_count, obs_error):
    mem_dev, tok_dev, width = hidden_in.shape
    variables, lon_dev, lat_all = observed.shape
    lon_all = lon_dev * lax.axis_size("tile")
    place = lax.axis_index("mem").astype(jnp.int32).reshape(1)
    lat_ids = jnp.arange(lat_all, dtype=jnp.int32) - lax.axis_index("tile")
    ratio = lat_ids.astype(F32) / (RAD + 1.0)
    lat_taper = jnp.where(jnp.abs(lat_ids) <= RAD, (1.0 - ratio * ratio) ** 2, 0.0)

    obs = jnp.concatenate([observed, obs_count[:1].astype(F32)], axis=0)
    obs = lax.all_to_all(obs, "tile", split_axis=2, concat_axis=1, tiled=True)
    obs = jnp.pad(obs.reshape(variables + 1, lon_all), ((0, VROWS - variables - 1), (0, 0)))
    err = jnp.pad(obs_error, (0, VROWS - variables), constant_values=1.0).reshape(VROWS, 1)

    fields = forecast(
        hidden_in.reshape(mem_dev * tok_dev, width),
        norm_gain.reshape(1, width),
        w_in,
        w_out,
        jnp.pad(w_dec, ((0, 2 * HROWS - variables), (0, 0))),
    )
    sectors = lax.all_to_all(fields, "mem", 0, 0, tiled=True)
    smooth, anomaly = pairs(place, sectors, obs, err, lat_all)
    rows = lax.all_to_all(smooth, "tile", 0, 0, tiled=True)
    increments = transform(lat_taper, rows, anomaly)
    back = lax.all_to_all(increments, "mem", 0, 0, tiled=True)
    return strips(back, variables).reshape(mem_dev, variables, tok_dev // lon_all, lon_all)


def solution(mesh):
    return jax.shard_map(
        body,
        mesh=mesh,
        in_specs=(
            P("mem", "tile", None),
            P(),
            P(),
            P(),
            P(),
            P(None, "tile", None),
            P(None, "tile", None),
            P(),
        ),
        out_specs=P("mem", None, "tile", None),
        check_vma=False,
    )
```

```python
import functools
import math

import jax
import jax.numpy as jnp
import numpy as np
from jax import lax
from jax.experimental import pallas as pl
from jax.experimental.pallas import tpu as pltpu
from jax.sharding import PartitionSpec as P

RAD = 6
NS_ITERS = 4
F32 = jnp.float32
BF16 = jnp.bfloat16

LANES = 128
VROWS = 72
HROWS = 40
HALO = 8
SECTOR = 32
MEMBERS = 32
GROUP = 4
DIAGS = MEMBERS // 2 + 1
ROWS = DIAGS + 1
FF_BLOCK = 1024
TOKEN_BLOCK = 512

UNSEEN = 1e30
COUNT = 3.0

LARGE = pltpu.CompilerParams(vmem_limit_bytes=60 * 2**20)
SMALL = pltpu.CompilerParams(vmem_limit_bytes=12 * 2**20)


def lanes_of(shape):
    return lax.broadcasted_iota(jnp.int32, shape, len(shape) - 1)


def gelu(h):
    inner = h * (math.sqrt(2.0 / math.pi) + (0.044715 * math.sqrt(2.0 / math.pi)) * (h * h))
    half = 0.5 * h
    return half + half * jnp.tanh(inner)


def forecast_kernel(x_ref, gain_ref, win_ref, wout_ref, wdec_ref, out_ref, normed, acc, decoder):
    step = pl.program_id(0)
    steps = pl.num_programs(0)
    tokens = x_ref.shape[0]
    blocks = tokens // TOKEN_BLOCK
    lon_all = tokens // GROUP

    @pl.when(step == 0)
    def _():
        gain = gain_ref[...].astype(F32).reshape(1, -1)
        decoder[...] = jnp.zeros_like(decoder)
        decoder[0 : wdec_ref.shape[0], :] = wdec_ref[...]
        for r in range(tokens // 128):
            xf = x_ref[pl.ds(r * 128, 128), :].astype(F32)
            centred = xf - jnp.mean(xf, axis=-1, keepdims=True)
            spread = jnp.mean(centred * centred, axis=-1, keepdims=True)
            normed[pl.ds(r * 128, 128), :] = (centred * lax.rsqrt(spread + 1e-05) * gain).astype(BF16)

    def up(r):
        return jnp.dot(
            normed[pl.ds(r * TOKEN_BLOCK, TOKEN_BLOCK), :], win_ref[...], preferred_element_type=F32
        )

    def run(first):
        hidden = up(0)
        for r in range(blocks):
            following = up(r + 1) if r + 1 < blocks else None
            down = jnp.dot(gelu(hidden).astype(BF16), wout_ref[...], preferred_element_type=F32)
            at = pl.ds(r * TOKEN_BLOCK, TOKEN_BLOCK)
            if first:
                acc[at, :] = down
            else:
                acc[at, :] += down
            hidden = following

    @pl.when(step == 0)
    def _():
        run(True)

    @pl.when(step > 0)
    def _():
        run(False)

    @pl.when(step == steps - 1)
    def _():
        acc[...] = x_ref[...].astype(F32) + acc[...]
        wdec = decoder[...]
        contract = (((1,), (1,)), ((), ()))
        for i in range(lon_all // SECTOR):
            main, halo = [], []
            for m in range(GROUP):
                base = m * lon_all
                main.append(acc[pl.ds(base + SECTOR * i, SECTOR), :])
                halo.append(acc[pl.ds(base + (SECTOR * i - HALO) % lon_all, HALO), :])
                halo.append(acc[pl.ds(base + (SECTOR * (i + 1)) % lon_all, HALO), :])
            main = jnp.concatenate(main, axis=0).astype(BF16)
            halo = jnp.concatenate(halo, axis=0).astype(BF16)
            main = lax.dot_general(wdec, main, contract, preferred_element_type=F32)
            halo = lax.dot_general(wdec, halo, contract, preferred_element_type=F32)
            halo = jnp.concatenate([halo[:HROWS], halo[HROWS:]], axis=1)
            out_ref[i] = jnp.concatenate([main[:VROWS], halo], axis=0).astype(BF16)


def forecast(x, gain, w_in, w_out, w_dec):
    tokens, width = x.shape
    hidden = w_in.shape[1]
    sectors = tokens // GROUP // SECTOR
    return pl.pallas_call(
        forecast_kernel,
        grid=(hidden // FF_BLOCK,),
        in_specs=[
            pl.BlockSpec((tokens, width), lambda s: (0, 0)),
            pl.BlockSpec((width,), lambda s: (0,)),
            pl.BlockSpec((width, FF_BLOCK), lambda s: (0, s)),
            pl.BlockSpec((FF_BLOCK, width), lambda s: (s, 0)),
            pl.BlockSpec(w_dec.shape, lambda s: (0, 0)),
        ],
        out_specs=pl.BlockSpec((sectors, VROWS + HROWS, LANES), lambda s: (0, 0, 0)),
        out_shape=jax.ShapeDtypeStruct((sectors, VROWS + HROWS, LANES), BF16),
        scratch_shapes=[
            pltpu.VMEM((tokens, width), BF16),
            pltpu.VMEM((tokens, width), F32),
            pltpu.VMEM((2 * HROWS, width), BF16),
        ],
        compiler_params=LARGE,
        cost_estimate=pl.CostEstimate(
            flops=4 * tokens * width * hidden, bytes_accessed=4 * width * hidden, transcendentals=0
        ),
        name="forecast",
    )(x, gain, w_in, w_out, w_dec)


def copies_over_lanes(tile, width):
    while width < LANES:
        tile = tile + pltpu.roll(tile, width, 1)
        width *= 2
    return tile


def sum_over_groups(tile, width):
    while width < LANES:
        tile = tile + pltpu.roll(tile, width, 1)
        width *= 2
    return tile


def shifted_tile(tiles, index, shift, width):
    move = shift * width
    if not move:
        return tiles(index)
    here = pltpu.roll(tiles(index), LANES - move, 1)
    there = pltpu.roll(tiles(index + 1), LANES - move, 1)
    return jnp.where(lanes_of(here.shape) < LANES - move, here, there)


def pair_sums(fields, observed, inv_count, width, weighted, moved, anomalies, put):
    count = len(fields)
    per = LANES // width
    total = fields[0]
    for tile in fields[1:]:
        total = total + tile
    mean = sum_over_groups(total, width) / MEMBERS
    for k in range(count):
        anomaly = fields[k] - mean
        if anomalies is not None:
            anomalies[k] = anomaly
        weighted[k] = (anomaly * inv_count).astype(BF16).astype(F32)
        moved[0, k] = anomaly.astype(BF16).astype(F32)
    for t in range(1, per):
        for k in range(count):
            moved[t, k] = shifted_tile(lambda j: moved[0, j % count], k, t, width)
    innovation = observed - mean
    for k in range(count):
        put(DIAGS, k, jnp.sum(weighted[k] * innovation, axis=0, keepdims=True))
    for s in range(DIAGS):
        on, t = divmod(s, per)
        for k in range(count):
            put(s, k, jnp.sum(weighted[k] * moved[t, (k + on) % count], axis=0, keepdims=True))


def pairs_kernel(
    place_ref, recv_ref, obs_ref, err_ref, taper_ref, out_ref, anom_ref,
    wide, weighted, moved, weighted_halo, moved_halo, sums,
):
    tiles = recv_ref.shape[0]
    lon_all, variables = obs_ref.shape
    wide[...] = jnp.zeros_like(wide)
    wide[0:lon_all, 0:variables] = obs_ref[...]
    wide[lon_all : lon_all + 1, 0:variables] = err_ref[...].reshape(1, variables)
    start = place_ref[0] * SECTOR

    def columns(at, count):
        return wide[pl.ds(pl.multiple_of(lax.rem(at + lon_all, lon_all), HALO), count), :]

    around = [columns(start - HALO, HALO), columns(start + SECTOR, HALO)]
    obs_main = jnp.concatenate([columns(start, SECTOR)] * GROUP, axis=0).T[:VROWS]
    obs_halo = jnp.concatenate(around * (LANES // (2 * HALO)), axis=0).T[:VROWS]
    err = jnp.broadcast_to(wide[lon_all : lon_all + 1, :], (LANES, LANES)).T[:VROWS]
    is_variable = lax.broadcasted_iota(jnp.int32, err.shape, 0) < variables
    each = jnp.where(is_variable, COUNT / (err * err), 0.0)
    prec_main = jnp.where(obs_main < 0.5 * UNSEEN, each, 0.0)
    prec_halo = jnp.where(obs_halo < 0.5 * UNSEEN, each, 0.0)

    sums[...] = jnp.zeros_like(sums)

    def put_main(s, k, row):
        sums[pl.ds(s * tiles + k, 1), 0:LANES] = row

    def put_halo(s, k, row):
        sums[pl.ds(s * tiles + 2 * k, 1), LANES : 2 * LANES] = row
        sums[pl.ds(s * tiles + 2 * k + 1, 1), 2 * LANES : 3 * LANES] = row

    fields, halos = [], []
    for m in range(tiles):
        both = recv_ref[m].astype(F32)
        fields.append(both[:VROWS])
        halos.append(both[VROWS:])
    left = lanes_of((HROWS, LANES)) < LANES // 2
    halo_fields = []
    for h in range(tiles // 2):
        a, b = halos[2 * h], halos[2 * h + 1]
        upper = jnp.where(left, a, pltpu.roll(b, LANES // 2, 1))
        lower = jnp.where(left, pltpu.roll(a, LANES // 2, 1), b)
        halo_fields.append(jnp.concatenate([upper, lower], axis=0)[:VROWS])
    pair_sums(fields, obs_main, prec_main, SECTOR, weighted, moved, anom_ref, put_main)
    pair_sums(halo_fields, obs_halo, prec_halo, 2 * HALO, weighted_halo, moved_halo, None, put_halo)
    smooth = jnp.dot(
        sums[...], taper_ref[...], precision=lax.Precision.HIGHEST, preferred_element_type=F32
    ).astype(BF16)
    for a in range(out_ref.shape[0]):
        out_ref[a] = smooth


def taper_of(offset):
    offset = np.asarray(offset, np.float32)
    ratio = offset / np.float32(RAD + 1.0)
    return np.where(np.abs(offset) <= RAD, (1.0 - ratio * ratio) ** 2, 0.0).astype(np.float32)


def longitude_taper():
    out_member, out_col = np.divmod(np.arange(LANES), SECTOR)
    main_member, main_col = np.divmod(np.arange(LANES), SECTOR)
    halo_member, halo_place = np.divmod(np.arange(LANES), 2 * HALO)
    halo_col = np.where(halo_place < HALO, halo_place - HALO, halo_place - HALO + SECTOR)
    parts = []
    for member, col in (
        (main_member, main_col), (halo_member, halo_col), (halo_member - GROUP, halo_col)
    ):
        same = member[:, None] == out_member[None, :]
        parts.append(np.where(same, taper_of(col[:, None] - out_col[None, :]), 0.0))
    return jnp.asarray(np.concatenate(parts, axis=0).astype(np.float32))


def pairs(place, recv, obs, err, n_rows):
    tiles = recv.shape[0]
    full = pl.BlockSpec(memory_space=pltpu.VMEM)
    return pl.pallas_call(
        pairs_kernel,
        in_specs=[pl.BlockSpec(memory_space=pltpu.SMEM), full, full, full, full],
        out_specs=(full, full),
        out_shape=(
            jax.ShapeDtypeStruct((n_rows, ROWS * tiles, LANES), BF16),
            jax.ShapeDtypeStruct((tiles, VROWS, LANES), F32),
        ),
        scratch_shapes=[
            pltpu.VMEM((obs.shape[0] + 8, LANES), F32),
            pltpu.VMEM((tiles, VROWS, LANES), F32),
            pltpu.VMEM((LANES // SECTOR, tiles, VROWS, LANES), F32),
            pltpu.VMEM((tiles // 2, VROWS, LANES), F32),
            pltpu.VMEM((LANES // (2 * HALO), tiles // 2, VROWS, LANES), F32),
            pltpu.VMEM((ROWS * tiles, 3 * LANES), F32),
        ],
        compiler_params=SMALL,
        name="pairs",
    )(place, recv, obs, err, longitude_taper())


def on_by(x, n):
    sub, t = divmod(n % MEMBERS, GROUP)
    if t:
        move = LANES - SECTOR * t
        x = pltpu.roll(x, move, 1)
        x = jnp.where(lanes_of(x.shape) < move, x, pltpu.roll(x, 7, 0))
    if sub:
        x = pltpu.roll(x, 8 - sub, 0)
    return x


def shifted_sum(term):
    total = None
    for t in range(GROUP - 1, -1, -1):
        inner = None
        for a in range(MEMBERS // GROUP - 1, -1, -1):
            part = term(GROUP * a + t)
            inner = part if inner is None else on_by(inner, GROUP) + part
        total = inner if total is None else on_by(total, 1) + inner
    return total


def product(left, right, out, scale=None, shift=None):
    for s in range(DIAGS):
        value = shifted_sum(lambda t: left[(-t) % MEMBERS] * right[(s - t) % MEMBERS])
        if scale is not None:
            value = scale * value
            if s == 0:
                value = value + shift
        out[s] = value
    mirror(out)


def mirror(out):
    for s in range(1, MEMBERS - DIAGS + 1):
        out[MEMBERS - s] = on_by(out[s], -s)


def transform_kernel(lat_ref, recv_ref, anom_ref, out_ref, bank, moved, coeff):
    rows = recv_ref.shape[0]
    tiles = anom_ref.shape[0]
    local = lat_ref[0] * recv_ref[0].astype(F32)
    for b in range(1, rows):
        local = local + lat_ref[b] * recv_ref[b].astype(F32)
    diag = [local[s * tiles : (s + 1) * tiles] for s in range(ROWS)]
    innov = diag[DIAGS]
    diag[0] = diag[0] + (MEMBERS - 1.0)
    gram, root, inv_root, corr = bank.at[0], bank.at[1], bank.at[2], bank.at[3]
    other_root, other_inv = bank.at[4], bank.at[5]
    square = None
    for s in range(DIAGS):
        part = diag[s] * diag[s]
        if 0 < s < DIAGS - 1:
            part = part + part
        square = part if square is None else square + part
    square = jnp.broadcast_to(jnp.sum(square, axis=0, keepdims=True), square.shape)
    frob = jnp.sqrt(sum_over_groups(square, SECTOR))
    inv_frob = 1.0 / frob
    for s in range(DIAGS):
        gram[s] = diag[s] * inv_frob
    mirror(gram)
    for s in range(MEMBERS):
        inv_root[s] = -0.5 * gram[s] + (1.5 if s == 0 else 0.0)
    product(gram, inv_root, root)
    for sweep in range(1, NS_ITERS):
        product(inv_root, root, corr, -0.5, 1.5)
        if sweep < NS_ITERS - 1:
            product(root, corr, other_root)
        product(corr, inv_root, other_inv)
        root, other_root = other_root, root
        inv_root, other_inv = other_inv, inv_root
    half = shifted_sum(lambda t: inv_root[(-t) % MEMBERS] * innov)
    mean_weights = shifted_sum(lambda t: inv_root[(-t) % MEMBERS] * half) * inv_frob
    factor = math.sqrt(MEMBERS - 1.0) / jnp.sqrt(frob)
    for s in range(MEMBERS):
        value = inv_root[s] * factor + on_by(mean_weights, s)
        coeff[pl.ds(s * tiles, tiles), :] = value.astype(BF16).astype(F32)
    for k in range(tiles):
        moved[0, k] = anom_ref[k].astype(BF16).astype(F32)
    for t in range(1, GROUP):
        for k in range(tiles):
            moved[t, k] = shifted_tile(lambda j: moved[0, j % tiles], k, t, SECTOR)
    for k in range(tiles):
        mixed = None
        for s in range(MEMBERS):
            on, t = divmod(s, GROUP)
            part = moved[t, (k + on) % tiles] * coeff[pl.ds(s * tiles + k, 1), :]
            mixed = part if mixed is None else mixed + part
        out_ref[k] = (mixed - anom_ref[k]).astype(BF16)


def transform(lat_taper, recv, anomaly):
    tiles = anomaly.shape[0]
    full = pl.BlockSpec(memory_space=pltpu.VMEM)
    return pl.pallas_call(
        transform_kernel,
        in_specs=[pl.BlockSpec(memory_space=pltpu.SMEM), full, full],
        out_specs=full,
        out_shape=jax.ShapeDtypeStruct((tiles, VROWS, LANES), BF16),
        scratch_shapes=[
            pltpu.VMEM((6, MEMBERS, tiles, LANES), F32),
            pltpu.VMEM((GROUP, tiles, VROWS, LANES), F32),
            pltpu.VMEM((MEMBERS * tiles, LANES), F32),
        ],
        compiler_params=SMALL,
        name="transform",
    )(lat_taper, recv, anomaly)


def strips_kernel(recv_ref, out_ref):
    tiles = recv_ref.shape[0]
    variables = out_ref.shape[1]
    parts = [recv_ref[i].astype(F32) for i in range(tiles)]
    group = lanes_of(parts[0].shape) // SECTOR
    for m in range(GROUP):
        for c in range(tiles // GROUP):
            tile = None
            for j in range(GROUP):
                piece = parts[GROUP * c + j]
                if j != m:
                    piece = pltpu.roll(piece, (SECTOR * (j - m)) % LANES, 1)
                tile = piece if tile is None else jnp.where(group == j, piece, tile)
            out_ref[m, :, 0, pl.ds(c * LANES, LANES)] = tile[:variables]


def strips(recv, variables):
    tiles = recv.shape[0]
    full = pl.BlockSpec(memory_space=pltpu.VMEM)
    return pl.pallas_call(
        strips_kernel,
        in_specs=[full],
        out_specs=full,
        out_shape=jax.ShapeDtypeStruct((GROUP, variables, 1, tiles * SECTOR), F32),
        compiler_params=SMALL,
        name="strips",
    )(recv)


def body(hidden_in, norm_gain, w_in, w_out, w_dec, observed, obs_count, obs_error):
    mem_dev, tok_dev, width = hidden_in.shape
    variables, lon_dev, lat_all = observed.shape
    lon_all = lon_dev * lax.axis_size("tile")
    place = lax.axis_index("mem").astype(jnp.int32).reshape(1)
    lat_ids = jnp.arange(lat_all, dtype=jnp.int32) - lax.axis_index("tile")
    ratio = lat_ids.astype(F32) / (RAD + 1.0)
    lat_taper = jnp.where(jnp.abs(lat_ids) <= RAD, (1.0 - ratio * ratio) ** 2, 0.0)

    seen = jnp.where(obs_count > 0, observed, UNSEEN)
    obs = lax.all_to_all(jnp.transpose(seen, (2, 1, 0)), "tile", 0, 1, tiled=True)

    fields = forecast(
        hidden_in.reshape(mem_dev * tok_dev, width),
        norm_gain,
        w_in,
        w_out,
        w_dec,
    )
    sectors = lax.all_to_all(fields, "mem", 0, 0, tiled=True)
    smooth, anomaly = pairs(place, sectors, obs.reshape(lon_all, variables), obs_error, lat_all)
    rows = lax.all_to_all(smooth, "tile", 0, 0, tiled=True)
    increments = transform(lat_taper, rows, anomaly)
    back = lax.all_to_all(increments, "mem", 0, 0, tiled=True)
    return strips(back, variables)


def solution(mesh):
    return jax.shard_map(
        body,
        mesh=mesh,
        in_specs=(
            P("mem", "tile", None),
            P(),
            P(),
            P(),
            P(),
            P(None, "tile", None),
            P(None, "tile", None),
            P(),
        ),
        out_specs=P("mem", None, "tile", None),
        check_vma=False,
    )
```

```python
import functools
import math

import jax
import jax.numpy as jnp
import numpy as np
from jax import lax
from jax.experimental import pallas as pl
from jax.experimental.pallas import tpu as pltpu
from jax.sharding import PartitionSpec as P

RAD = 6
NS_ITERS = 4
F32 = jnp.float32
BF16 = jnp.bfloat16

LANES = 128
VROWS = 72
HROWS = 40
CORES = 2
HALF = 16
HALO = 8
WINDOW = HALF + 2 * HALO
POINTS = CORES * HALF
MEMBERS = 32
GROUP = 4
DIAGS = MEMBERS // 2 + 1
ROWS = DIAGS + 1
FF_BLOCK = 1024
TOKEN_BLOCK = 512

UNSEEN = 1e30
COUNT = 3.0

LARGE = pltpu.CompilerParams(vmem_limit_bytes=60 * 2**20)
SMALL = pltpu.CompilerParams(vmem_limit_bytes=12 * 2**20)


def lanes_of(shape):
    return lax.broadcasted_iota(jnp.int32, shape, len(shape) - 1)


def gelu(h):
    inner = h * (math.sqrt(2.0 / math.pi) + (0.044715 * math.sqrt(2.0 / math.pi)) * (h * h))
    half = 0.5 * h
    return half + half * jnp.tanh(inner)


def forecast_kernel(x_ref, gain_ref, win_ref, wout_ref, wdec_ref, out_ref, normed, acc, decoder):
    step = pl.program_id(0)
    steps = pl.num_programs(0)
    tokens = x_ref.shape[0]
    blocks = tokens // TOKEN_BLOCK
    lon_all = tokens // GROUP

    @pl.when(step == 0)
    def _():
        gain = gain_ref[...].astype(F32).reshape(1, -1)
        decoder[...] = jnp.zeros_like(decoder)
        decoder[0 : wdec_ref.shape[0], :] = wdec_ref[...]
        for r in range(tokens // 128):
            xf = x_ref[pl.ds(r * 128, 128), :].astype(F32)
            centred = xf - jnp.mean(xf, axis=-1, keepdims=True)
            spread = jnp.mean(centred * centred, axis=-1, keepdims=True)
            normed[pl.ds(r * 128, 128), :] = (centred * lax.rsqrt(spread + 1e-05) * gain).astype(BF16)

    def up(r):
        return jnp.dot(
            normed[pl.ds(r * TOKEN_BLOCK, TOKEN_BLOCK), :], win_ref[...], preferred_element_type=F32
        )

    def run(first):
        hidden = up(0)
        for r in range(blocks):
            following = up(r + 1) if r + 1 < blocks else None
            down = jnp.dot(gelu(hidden).astype(BF16), wout_ref[...], preferred_element_type=F32)
            at = pl.ds(r * TOKEN_BLOCK, TOKEN_BLOCK)
            if first:
                acc[at, :] = down
            else:
                acc[at, :] += down
            hidden = following

    @pl.when(step == 0)
    def _():
        run(True)

    @pl.when(step > 0)
    def _():
        run(False)

    @pl.when(step == steps - 1)
    def _():
        acc[...] = x_ref[...].astype(F32) + acc[...]
        wdec = decoder[...]
        contract = (((1,), (1,)), ((), ()))
        for h in range(lon_all // HALF):
            window = []
            for m in range(GROUP):
                for at in (HALF * h, HALF * (h + 1)):
                    window.append(acc[pl.ds(m * lon_all + at % lon_all, HALF), :])
            window = jnp.concatenate(window, axis=0).astype(BF16)
            decoded = lax.dot_general(wdec, window, contract, preferred_element_type=F32)
            out_ref[h] = decoded[:VROWS].astype(BF16)


def forecast(x, gain, w_in, w_out, w_dec):
    tokens, width = x.shape
    hidden = w_in.shape[1]
    halves = tokens // GROUP // HALF
    return pl.pallas_call(
        forecast_kernel,
        grid=(hidden // FF_BLOCK,),
        in_specs=[
            pl.BlockSpec((tokens, width), lambda s: (0, 0)),
            pl.BlockSpec((width,), lambda s: (0,)),
            pl.BlockSpec((width, FF_BLOCK), lambda s: (0, s)),
            pl.BlockSpec((FF_BLOCK, width), lambda s: (s, 0)),
            pl.BlockSpec(w_dec.shape, lambda s: (0, 0)),
        ],
        out_specs=pl.BlockSpec((halves, VROWS, LANES), lambda s: (0, 0, 0)),
        out_shape=jax.ShapeDtypeStruct((halves, VROWS, LANES), BF16),
        scratch_shapes=[
            pltpu.VMEM((tokens, width), BF16),
            pltpu.VMEM((tokens, width), F32),
            pltpu.VMEM((2 * HROWS, width), BF16),
        ],
        compiler_params=LARGE,
        cost_estimate=pl.CostEstimate(
            flops=4 * tokens * width * hidden, bytes_accessed=4 * width * hidden, transcendentals=0
        ),
        name="forecast",
    )(x, gain, w_in, w_out, w_dec)


def sum_over_groups(tile, width):
    while width < LANES:
        tile = tile + pltpu.roll(tile, width, 1)
        width *= 2
    return tile


def shifted_tile(tiles, index, shift, width):
    move = shift * width
    if not move:
        return tiles(index)
    here = pltpu.roll(tiles(index), LANES - move, 1)
    there = pltpu.roll(tiles(index + 1), LANES - move, 1)
    return jnp.where(lanes_of(here.shape) < LANES - move, here, there)


def pair_sums(fields, observed, prec, width, weighted, moved, put):
    count = len(fields)
    per = LANES // width
    total = fields[0]
    for tile in fields[1:]:
        total = total + tile
    mean = sum_over_groups(total, width) / MEMBERS
    anomalies = []
    for k in range(count):
        anomaly = fields[k] - mean
        anomalies.append(anomaly)
        weighted[k] = (anomaly * prec).astype(BF16).astype(F32)
        moved[0, k] = anomaly.astype(BF16).astype(F32)
    for t in range(1, per):
        for k in range(count):
            moved[t, k] = shifted_tile(lambda j: moved[0, j % count], k, t, width)
    innovation = observed - mean
    for k in range(count):
        put(DIAGS, k, jnp.sum(weighted[k] * innovation, axis=0, keepdims=True))
    for s in range(DIAGS):
        on, t = divmod(s, per)
        for k in range(count):
            put(s, k, jnp.sum(weighted[k] * moved[t, (k + on) % count], axis=0, keepdims=True))
    return anomalies


def pairs_kernel(
    recv_ref, west_ref, east_ref, err_ref, taper_ref, out_ref, anom_ref,
    wide, weighted, moved, sums,
):
    tiles = recv_ref.shape[0] // CORES
    variables = west_ref.shape[2]
    wide[...] = jnp.zeros_like(wide)
    wide[0:1, 0:variables] = err_ref[...].reshape(1, variables)
    err = jnp.broadcast_to(wide[0:1, :], (LANES, LANES)).T[:VROWS]
    is_variable = lax.broadcasted_iota(jnp.int32, err.shape, 0) < variables
    each = jnp.where(is_variable, COUNT / (err * err), 0.0)

    anomalies = []
    for r in range(CORES):
        wide[0:HALF, 0:variables] = west_ref[r]
        wide[HALF:WINDOW, 0:variables] = east_ref[r]
        obs = jnp.concatenate([wide[...]] * GROUP, axis=0).T[:VROWS]
        prec = jnp.where(obs < 0.5 * UNSEEN, each, 0.0)

        def put(s, k, row):
            sums[pl.ds(s * tiles + k, 1), r * LANES : (r + 1) * LANES] = row

        fields = [recv_ref[CORES * m + r].astype(F32) for m in range(tiles)]
        anomalies.append(
            pair_sums(fields, obs, prec, WINDOW, weighted.at[r], moved.at[r], put)
        )
    lower = lanes_of((VROWS, LANES)) % POINTS < HALF
    for k in range(tiles):
        anom_ref[k] = jnp.where(
            lower,
            pltpu.roll(anomalies[0][k], LANES - HALO, 1),
            pltpu.roll(anomalies[1][k], HALF - HALO, 1),
        )
    smooth = jnp.dot(
        sums[...], taper_ref[...], precision=lax.Precision.HIGHEST, preferred_element_type=F32
    ).astype(BF16)
    for c in range(out_ref.shape[0]):
        out_ref[c] = smooth


def taper_of(offset):
    offset = np.asarray(offset, np.float32)
    ratio = offset / np.float32(RAD + 1.0)
    return np.where(np.abs(offset) <= RAD, (1.0 - ratio * ratio) ** 2, 0.0).astype(np.float32)


def longitude_taper():
    lat, rest = np.divmod(np.arange(CORES * LANES), LANES)
    member, col = np.divmod(rest, WINDOW)
    out_member, rest = np.divmod(np.arange(LANES), POINTS)
    out_lat, out_col = np.divmod(rest, HALF)
    same = (lat[:, None] == out_lat[None, :]) & (member[:, None] == out_member[None, :])
    weight = taper_of(col[:, None] - HALO - out_col[None, :])
    return jnp.asarray(np.where(same, weight, 0.0).astype(np.float32))


def pairs(recv, obs, err, chips):
    tiles = recv.shape[0] // CORES
    full = pl.BlockSpec(memory_space=pltpu.VMEM)
    return pl.pallas_call(
        pairs_kernel,
        in_specs=[full] * 5,
        out_specs=(full, full),
        out_shape=(
            jax.ShapeDtypeStruct((chips, ROWS * tiles, LANES), BF16),
            jax.ShapeDtypeStruct((tiles, VROWS, LANES), F32),
        ),
        scratch_shapes=[
            pltpu.VMEM((WINDOW, LANES), F32),
            pltpu.VMEM((CORES, tiles, VROWS, LANES), F32),
            pltpu.VMEM((CORES, LANES // WINDOW, tiles, VROWS, LANES), F32),
            pltpu.VMEM((ROWS * tiles, CORES * LANES), F32),
        ],
        compiler_params=SMALL,
        name="pairs",
    )(recv, *obs, err, longitude_taper())


def on_by(x, n):
    sub, t = divmod(n % MEMBERS, GROUP)
    if t:
        move = LANES - POINTS * t
        x = pltpu.roll(x, move, 1)
        x = jnp.where(lanes_of(x.shape) < move, x, pltpu.roll(x, 7, 0))
    if sub:
        x = pltpu.roll(x, 8 - sub, 0)
    return x


def shifted_sum(term):
    total = None
    for t in range(GROUP - 1, -1, -1):
        inner = None
        for a in range(MEMBERS // GROUP - 1, -1, -1):
            part = term(GROUP * a + t)
            inner = part if inner is None else on_by(inner, GROUP) + part
        total = inner if total is None else on_by(total, 1) + inner
    return total


def product(left, right, out, scale=None, shift=None):
    for s in range(DIAGS):
        value = shifted_sum(lambda t: left[(-t) % MEMBERS] * right[(s - t) % MEMBERS])
        if scale is not None:
            value = scale * value
            if s == 0:
                value = value + shift
        out[s] = value
    mirror(out)


def mirror(out):
    for s in range(1, MEMBERS - DIAGS + 1):
        out[MEMBERS - s] = on_by(out[s], -s)


def latitude_weight(offset):
    ratio = offset.astype(F32) * (1.0 / (RAD + 1.0))
    return jnp.where(jnp.abs(offset) <= RAD, (1.0 - ratio * ratio) * (1.0 - ratio * ratio), 0.0)


def transform_kernel(place_ref, recv_ref, anom_ref, out_ref, bank, moved, coeff):
    chips = recv_ref.shape[0]
    tiles = anom_ref.shape[0]
    same, south, north = None, None, None
    for c in range(chips):
        sums = recv_ref[c].astype(F32)
        offset = CORES * (place_ref[0] - c)
        parts = [latitude_weight(offset + d) * sums for d in (0, -1, 1)]
        if c == 0:
            same, south, north = parts
        else:
            same, south, north = same + parts[0], south + parts[1], north + parts[2]
    lower = lanes_of(same.shape) % POINTS < HALF
    local = same + jnp.where(
        lower, pltpu.roll(south, LANES - HALF, 1), pltpu.roll(north, HALF, 1)
    )
    diag = [local[s * tiles : (s + 1) * tiles] for s in range(ROWS)]
    innov = diag[DIAGS]
    diag[0] = diag[0] + (MEMBERS - 1.0)
    gram, root, inv_root, corr = bank.at[0], bank.at[1], bank.at[2], bank.at[3]
    other_root, other_inv = bank.at[4], bank.at[5]
    square = None
    for s in range(DIAGS):
        part = diag[s] * diag[s]
        if 0 < s < DIAGS - 1:
            part = part + part
        square = part if square is None else square + part
    square = jnp.broadcast_to(jnp.sum(square, axis=0, keepdims=True), square.shape)
    frob = jnp.sqrt(sum_over_groups(square, POINTS))
    inv_frob = 1.0 / frob
    for s in range(DIAGS):
        gram[s] = diag[s] * inv_frob
    mirror(gram)
    for s in range(MEMBERS):
        inv_root[s] = -0.5 * gram[s] + (1.5 if s == 0 else 0.0)
    product(gram, inv_root, root)
    for sweep in range(1, NS_ITERS):
        product(inv_root, root, corr, -0.5, 1.5)
        if sweep < NS_ITERS - 1:
            product(root, corr, other_root)
        product(corr, inv_root, other_inv)
        root, other_root = other_root, root
        inv_root, other_inv = other_inv, inv_root
    half = shifted_sum(lambda t: inv_root[(-t) % MEMBERS] * innov)
    mean_weights = shifted_sum(lambda t: inv_root[(-t) % MEMBERS] * half) * inv_frob
    factor = math.sqrt(MEMBERS - 1.0) / jnp.sqrt(frob)
    for s in range(MEMBERS):
        value = inv_root[s] * factor + on_by(mean_weights, s)
        coeff[pl.ds(s * tiles, tiles), :] = value.astype(BF16).astype(F32)
    for k in range(tiles):
        moved[0, k] = anom_ref[k].astype(BF16).astype(F32)
    for t in range(1, GROUP):
        for k in range(tiles):
            moved[t, k] = shifted_tile(lambda j: moved[0, j % tiles], k, t, POINTS)
    for k in range(tiles):
        mixed = None
        for s in range(MEMBERS):
            on, t = divmod(s, GROUP)
            part = moved[t, (k + on) % tiles] * coeff[pl.ds(s * tiles + k, 1), :]
            mixed = part if mixed is None else mixed + part
        mixed = mixed - anom_ref[k]
        low = mixed[:HROWS]
        high = jnp.concatenate([mixed[HROWS:], jnp.zeros((2 * HROWS - VROWS, LANES), F32)], axis=0)
        first = lanes_of(low.shape) % POINTS < HALF
        out_ref[CORES * k] = jnp.where(first, low, pltpu.roll(high, HALF, 1)).astype(BF16)
        out_ref[CORES * k + 1] = jnp.where(first, pltpu.roll(low, LANES - HALF, 1), high).astype(BF16)


def transform(place, recv, anomaly):
    tiles = anomaly.shape[0]
    full = pl.BlockSpec(memory_space=pltpu.VMEM)
    return pl.pallas_call(
        transform_kernel,
        in_specs=[pl.BlockSpec(memory_space=pltpu.SMEM), full, full],
        out_specs=full,
        out_shape=jax.ShapeDtypeStruct((CORES * tiles, HROWS, LANES), BF16),
        scratch_shapes=[
            pltpu.VMEM((6, MEMBERS, tiles, LANES), F32),
            pltpu.VMEM((GROUP, tiles, VROWS, LANES), F32),
            pltpu.VMEM((MEMBERS * tiles, LANES), F32),
        ],
        compiler_params=SMALL,
        name="transform",
    )(place, recv, anomaly)


def strips_kernel(recv_ref, out_ref):
    halves = recv_ref.shape[0]
    variables = out_ref.shape[1]
    per = LANES // HALF
    parts = [recv_ref[h].astype(F32) for h in range(halves)]
    group = lax.rem(lanes_of(parts[0].shape) + (LANES - HALO), LANES) // HALF
    first = lanes_of(parts[0].shape) < HALO
    for m in range(GROUP):
        for side in range(2):
            tiles = []
            for c in range(halves // per):
                tile = None
                for j in range(per):
                    piece = parts[per * c + j]
                    move = (HALF * (j - side) - POINTS * m + HALO) % LANES
                    if move:
                        piece = pltpu.roll(piece, move, 1)
                    tile = piece if tile is None else jnp.where(group == j, piece, tile)
                tiles.append(tile)
            for c in range(len(tiles)):
                tile = jnp.where(first, tiles[c - 1], tiles[c])
                at = pl.ds(c * LANES, LANES)
                if side == 0:
                    out_ref[m, 0:HROWS, 0, at] = tile
                else:
                    out_ref[m, HROWS:variables, 0, at] = tile[: variables - HROWS]


def strips(recv, variables):
    halves = recv.shape[0]
    full = pl.BlockSpec(memory_space=pltpu.VMEM)
    return pl.pallas_call(
        strips_kernel,
        in_specs=[full],
        out_specs=full,
        out_shape=jax.ShapeDtypeStruct((GROUP, variables, 1, halves * HALF), F32),
        compiler_params=SMALL,
        name="strips",
    )(recv)


def body(hidden_in, norm_gain, w_in, w_out, w_dec, observed, obs_count, obs_error):
    mem_dev, tok_dev, width = hidden_in.shape
    variables, lon_dev, lat_all = observed.shape
    n_mem, n_tile = lax.axis_size("mem"), lax.axis_size("tile")
    chips = n_tile // CORES
    mem, tile = lax.axis_index("mem"), lax.axis_index("tile")
    place = lax.div(tile, CORES).astype(jnp.int32).reshape(1)
    by_chip = [
        [m * n_tile + c * CORES + k for m in range(n_mem) for k in range(CORES)] for c in range(chips)
    ]
    by_core = [[c * CORES + k for c in range(chips)] for k in range(CORES)]

    seen = jnp.where(obs_count > 0, observed, UNSEEN)
    seen = lax.dynamic_slice_in_dim(seen, CORES * mem, CORES, 2)
    seen = jnp.transpose(seen, (2, 1, 0))

    def to_sector(part, move):
        pairs_of = []
        for m in range(n_mem):
            for j in range(n_tile):
                to = (j + move) % n_tile
                pairs_of.append((m * n_tile + j, to // CORES * n_tile + CORES * m + to % CORES))
        return lax.ppermute(part, ("mem", "tile"), pairs_of)

    obs = [to_sector(seen, 0), to_sector(seen, -1)]

    fields = forecast(
        hidden_in.reshape(mem_dev * tok_dev, width), norm_gain, w_in, w_out, w_dec
    )
    halves = lax.all_to_all(
        fields, ("mem", "tile"), 0, 0, tiled=True, axis_index_groups=by_chip
    )
    smooth, anomaly = pairs(halves, obs, obs_error, chips)
    rows = lax.all_to_all(smooth, "tile", 0, 0, tiled=True, axis_index_groups=by_core)
    increments = transform(place, rows, anomaly)
    back = lax.all_to_all(
        increments, ("mem", "tile"), 0, 0, tiled=True, axis_index_groups=by_chip
    )
    return strips(back, variables)


def solution(mesh):
    return jax.shard_map(
        body,
        mesh=mesh,
        in_specs=(
            P("mem", "tile", None),
            P(),
            P(),
            P(),
            P(),
            P(None, "tile", None),
            P(None, "tile", None),
            P(),
        ),
        out_specs=P("mem", None, "tile", None),
        check_vma=False,
    )
```

```python
import functools
import math

import jax
import jax.numpy as jnp
import numpy as np
from jax import lax
from jax.experimental import pallas as pl
from jax.experimental.pallas import tpu as pltpu
from jax.sharding import PartitionSpec as P

RAD = 6
NS_ITERS = 4
F32 = jnp.float32
BF16 = jnp.bfloat16

LANES = 128
VROWS = 72
HROWS = 40
CORES = 2
HALF = 16
HALO = 8
WINDOW = HALF + 2 * HALO
POINTS = CORES * HALF
MEMBERS = 32
GROUP = 4
DIAGS = MEMBERS // 2 + 1
ROWS = DIAGS + 1
FF_BLOCK = 1024
TOKEN_BLOCK = 512

UNSEEN = 1e30
COUNT = 3.0

LARGE = pltpu.CompilerParams(vmem_limit_bytes=60 * 2**20)
SMALL = pltpu.CompilerParams(vmem_limit_bytes=12 * 2**20)


def lanes_of(shape):
    return lax.broadcasted_iota(jnp.int32, shape, len(shape) - 1)


def gelu(h):
    inner = h * (math.sqrt(2.0 / math.pi) + (0.044715 * math.sqrt(2.0 / math.pi)) * (h * h))
    half = 0.5 * h
    return half + half * jnp.tanh(inner)


SENDS = (0, -1)


def served(mem, tile, move, ways):
    n_tile, n_y = ways
    half = lax.rem(tile + (n_tile + move), n_tile)
    to_mem = lax.div(half, CORES)
    z_lo, y = lax.div(mem, n_y), lax.rem(mem, n_y)
    to_z_lo, to_y = lax.div(to_mem, n_y), lax.rem(to_mem, n_y)
    chip = lax.div(tile, CORES)
    x, z_hi = lax.div(chip, 2), lax.rem(chip, 2)
    n_x = n_tile // (2 * CORES)
    to_x = lax.rem(x + 2 + to_y - y + 2 * n_x, n_x)
    to_z_hi = lax.rem(z_hi + z_lo + to_z_lo, 2)
    return half, 2 * to_x + to_z_hi


def served_here(mem, tile, move, ways):
    n_tile, n_y = ways
    half = (tile + n_tile + move) % n_tile
    to_mem = half // CORES
    z_lo, y = mem // n_y, mem % n_y
    to_z_lo, to_y = to_mem // n_y, to_mem % n_y
    chip = tile // CORES
    x, z_hi = chip // 2, chip % 2
    n_x = n_tile // (2 * CORES)
    to_x = (x + 2 + to_y - y) % n_x
    to_z_hi = (z_hi + z_lo + to_z_lo) % 2
    return half, 2 * to_x + to_z_hi


def forecast_kernel(
    place_ref, x_ref, gain_ref, win_ref, wout_ref, wdec_ref, obs_ref, count_ref, out_ref, west_ref, east_ref,
    normed, acc, decoder, *, n_y,
):
    step = pl.program_id(0)
    steps = pl.num_programs(0)
    tokens = x_ref.shape[0]
    blocks = tokens // TOKEN_BLOCK
    lon_all = tokens // GROUP

    @pl.when(step == 0)
    def _():
        gain = gain_ref[...].astype(F32).reshape(1, -1)
        n_tile = out_ref.shape[0]
        mem, tile = lax.div(place_ref[0], n_tile), lax.rem(place_ref[0], n_tile)
        for seen_ref, move in zip((west_ref, east_ref), SENDS):
            _, chip = served(mem, tile, move, (n_tile, n_y))
            for r in range(CORES):
                row = CORES * chip + r
                seen_ref[r] = jnp.where(count_ref[:, row, :] > 0, obs_ref[:, row, :], UNSEEN)
        decoder[...] = jnp.zeros_like(decoder)
        decoder[0 : wdec_ref.shape[0], :] = wdec_ref[...]
        for r in range(tokens // 128):
            xf = x_ref[pl.ds(r * 128, 128), :].astype(F32)
            centred = xf - jnp.mean(xf, axis=-1, keepdims=True)
            spread = jnp.mean(centred * centred, axis=-1, keepdims=True)
            normed[pl.ds(r * 128, 128), :] = (centred * lax.rsqrt(spread + 1e-05) * gain).astype(BF16)

    def up(r):
        return jnp.dot(
            normed[pl.ds(r * TOKEN_BLOCK, TOKEN_BLOCK), :], win_ref[...], preferred_element_type=F32
        )

    def run(first):
        hidden = up(0)
        for r in range(blocks):
            following = up(r + 1) if r + 1 < blocks else None
            down = jnp.dot(gelu(hidden).astype(BF16), wout_ref[...], preferred_element_type=F32)
            at = pl.ds(r * TOKEN_BLOCK, TOKEN_BLOCK)
            if first:
                acc[at, :] = down
            else:
                acc[at, :] += down
            hidden = following

    @pl.when(step == 0)
    def _():
        run(True)

    @pl.when(step > 0)
    def _():
        run(False)

    @pl.when(step == steps - 1)
    def _():
        acc[...] = x_ref[...].astype(F32) + acc[...]
        wdec = decoder[...]
        contract = (((1,), (1,)), ((), ()))
        for h in range(lon_all // HALF):
            window = []
            for m in range(GROUP):
                for at in (HALF * h, HALF * (h + 1)):
                    window.append(acc[pl.ds(m * lon_all + at % lon_all, HALF), :])
            window = jnp.concatenate(window, axis=0).astype(BF16)
            decoded = lax.dot_general(wdec, window, contract, preferred_element_type=F32)
            out_ref[h] = decoded[:VROWS].astype(BF16)


def forecast(place, n_y, x, gain, w_in, w_out, w_dec, observed, obs_count):
    tokens, width = x.shape
    hidden = w_in.shape[1]
    halves = tokens // GROUP // HALF
    lon_dev, _, variables = observed.shape
    whole = pl.BlockSpec(observed.shape, lambda s: (0, 0, 0))
    return pl.pallas_call(
        functools.partial(forecast_kernel, n_y=n_y),
        grid=(hidden // FF_BLOCK,),
        in_specs=[
            pl.BlockSpec(memory_space=pltpu.SMEM),
            pl.BlockSpec((tokens, width), lambda s: (0, 0)),
            pl.BlockSpec((width,), lambda s: (0,)),
            pl.BlockSpec((width, FF_BLOCK), lambda s: (0, s)),
            pl.BlockSpec((FF_BLOCK, width), lambda s: (s, 0)),
            pl.BlockSpec(w_dec.shape, lambda s: (0, 0)),
            whole,
            whole,
        ],
        out_specs=(
            pl.BlockSpec((halves, VROWS, LANES), lambda s: (0, 0, 0)),
            pl.BlockSpec((CORES, lon_dev, variables), lambda s: (0, 0, 0)),
            pl.BlockSpec((CORES, lon_dev, variables), lambda s: (0, 0, 0)),
        ),
        out_shape=(
            jax.ShapeDtypeStruct((halves, VROWS, LANES), BF16),
            jax.ShapeDtypeStruct((CORES, lon_dev, variables), F32),
            jax.ShapeDtypeStruct((CORES, lon_dev, variables), F32),
        ),
        scratch_shapes=[
            pltpu.VMEM((tokens, width), BF16),
            pltpu.VMEM((tokens, width), F32),
            pltpu.VMEM((2 * HROWS, width), BF16),
        ],
        compiler_params=LARGE,
        cost_estimate=pl.CostEstimate(
            flops=4 * tokens * width * hidden, bytes_accessed=4 * width * hidden, transcendentals=0
        ),
        name="forecast",
    )(place, x, gain, w_in, w_out, w_dec, observed, obs_count)


def sum_over_groups(tile, width):
    while width < LANES:
        tile = tile + pltpu.roll(tile, width, 1)
        width *= 2
    return tile


def shifted_tile(tiles, index, shift, width):
    move = shift * width
    if not move:
        return tiles(index)
    here = pltpu.roll(tiles(index), LANES - move, 1)
    there = pltpu.roll(tiles(index + 1), LANES - move, 1)
    return jnp.where(lanes_of(here.shape) < LANES - move, here, there)


def pair_sums(fields, prec, width, weighted, moved, put):
    count = len(fields)
    per = LANES // width
    total = fields[0]
    for tile in fields[1:]:
        total = total + tile
    mean = sum_over_groups(total, width) / MEMBERS
    anomalies = []
    for k in range(count):
        anomaly = fields[k] - mean
        anomalies.append(anomaly)
        weighted[k] = (anomaly * prec).astype(BF16).astype(F32)
        moved[0, k] = anomaly.astype(BF16).astype(F32)
    for t in range(1, per):
        for k in range(count):
            moved[t, k] = shifted_tile(lambda j: moved[0, j % count], k, t, width)
    for s in range(DIAGS):
        on, t = divmod(s, per)
        for k in range(count):
            put(s, k, jnp.sum(weighted[k] * moved[t, (k + on) % count], axis=0, keepdims=True))
    return mean, anomalies


def pairs_kernel(recv_ref, err_ref, sums, weighted, mean_ref, anom_ref, wide, moved):
    tiles = recv_ref.shape[0] // CORES
    variables = err_ref.shape[0]
    wide[...] = jnp.zeros_like(wide)
    wide[0:1, 0:variables] = err_ref[...].reshape(1, variables)
    err = jnp.broadcast_to(wide[0:1, :], (LANES, LANES)).T[:VROWS]
    is_variable = lax.broadcasted_iota(jnp.int32, err.shape, 0) < variables
    prec = jnp.where(is_variable, COUNT / (err * err), 0.0)

    sums[pl.ds(DIAGS * tiles, tiles), :] = jnp.zeros((tiles, CORES * LANES), F32)
    anomalies = []
    for r in range(CORES):

        def put(s, k, row):
            sums[pl.ds(s * tiles + k, 1), r * LANES : (r + 1) * LANES] = row

        fields = [recv_ref[CORES * m + r].astype(F32) for m in range(tiles)]
        mean, anomaly = pair_sums(fields, prec, WINDOW, weighted.at[r], moved.at[r], put)
        mean_ref[r] = mean
        anomalies.append(anomaly)
    lower = lanes_of((VROWS, LANES)) % POINTS < HALF
    for k in range(tiles):
        anom_ref[k] = jnp.where(
            lower,
            pltpu.roll(anomalies[0][k], LANES - HALO, 1),
            pltpu.roll(anomalies[1][k], HALF - HALO, 1),
        )


def smooth_kernel(sums_ref, weighted, mean_ref, west_ref, east_ref, taper_ref, out_ref, wide, sums):
    tiles = weighted.shape[1]
    variables = west_ref.shape[2]
    wide[...] = jnp.zeros_like(wide)
    for r in range(CORES):
        at = slice(r * LANES, (r + 1) * LANES)
        wide[0:HALF, 0:variables] = west_ref[r]
        wide[HALF:WINDOW, 0:variables] = east_ref[r]
        obs = jnp.concatenate([wide[...]] * GROUP, axis=0).T[:VROWS]
        is_seen = obs[0:1] < 0.5 * UNSEEN
        innovation = obs - mean_ref[r]
        diags = sums_ref[0 : DIAGS * tiles, at]
        sums[0 : DIAGS * tiles, at] = jnp.where(is_seen, diags, 0.0)
        for k in range(tiles):
            row = jnp.sum(weighted[r, k] * innovation, axis=0, keepdims=True)
            sums[pl.ds(DIAGS * tiles + k, 1), at] = jnp.where(is_seen, row, 0.0)
    smooth = jnp.dot(
        sums[...], taper_ref[...], precision=lax.Precision.HIGHEST, preferred_element_type=F32
    ).astype(BF16)
    for c in range(out_ref.shape[0]):
        out_ref[c] = smooth


def taper_of(offset):
    offset = np.asarray(offset, np.float32)
    ratio = offset / np.float32(RAD + 1.0)
    return np.where(np.abs(offset) <= RAD, (1.0 - ratio * ratio) ** 2, 0.0).astype(np.float32)


def longitude_taper():
    lat, rest = np.divmod(np.arange(CORES * LANES), LANES)
    member, col = np.divmod(rest, WINDOW)
    out_member, rest = np.divmod(np.arange(LANES), POINTS)
    out_lat, out_col = np.divmod(rest, HALF)
    same = (lat[:, None] == out_lat[None, :]) & (member[:, None] == out_member[None, :])
    weight = taper_of(col[:, None] - HALO - out_col[None, :])
    return jnp.asarray(np.where(same, weight, 0.0).astype(np.float32))


def pairs(recv, err):
    tiles = recv.shape[0] // CORES
    full = pl.BlockSpec(memory_space=pltpu.VMEM)
    return pl.pallas_call(
        pairs_kernel,
        in_specs=[full] * 2,
        out_specs=(full,) * 4,
        out_shape=(
            jax.ShapeDtypeStruct((ROWS * tiles, CORES * LANES), F32),
            jax.ShapeDtypeStruct((CORES, tiles, VROWS, LANES), F32),
            jax.ShapeDtypeStruct((CORES, VROWS, LANES), F32),
            jax.ShapeDtypeStruct((tiles, VROWS, LANES), F32),
        ),
        scratch_shapes=[
            pltpu.VMEM((8, LANES), F32),
            pltpu.VMEM((CORES, LANES // WINDOW, tiles, VROWS, LANES), F32),
        ],
        compiler_params=SMALL,
        name="pairs",
    )(recv, err)


def smooth(sums, weighted, mean, obs, chips):
    full = pl.BlockSpec(memory_space=pltpu.VMEM)
    return pl.pallas_call(
        smooth_kernel,
        in_specs=[full] * 6,
        out_specs=full,
        out_shape=jax.ShapeDtypeStruct((chips, sums.shape[0], LANES), BF16),
        scratch_shapes=[pltpu.VMEM((WINDOW, LANES), F32), pltpu.VMEM(sums.shape, F32)],
        compiler_params=SMALL,
        name="smooth",
    )(sums, weighted, mean, *obs, longitude_taper())


def on_by(x, n):
    sub, t = divmod(n % MEMBERS, GROUP)
    if t:
        move = LANES - POINTS * t
        x = pltpu.roll(x, move, 1)
        x = jnp.where(lanes_of(x.shape) < move, x, pltpu.roll(x, 7, 0))
    if sub:
        x = pltpu.roll(x, 8 - sub, 0)
    return x


def shifted_sum(term):
    total = None
    for t in range(GROUP - 1, -1, -1):
        inner = None
        for a in range(MEMBERS // GROUP - 1, -1, -1):
            part = term(GROUP * a + t)
            inner = part if inner is None else on_by(inner, GROUP) + part
        total = inner if total is None else on_by(total, 1) + inner
    return total


def product(left, right, out, scale=None, shift=None):
    for s in range(DIAGS):
        value = shifted_sum(lambda t: left[(-t) % MEMBERS] * right[(s - t) % MEMBERS])
        if scale is not None:
            value = scale * value
            if s == 0:
                value = value + shift
        out[s] = value
    mirror(out)


def mirror(out):
    for s in range(1, MEMBERS - DIAGS + 1):
        out[MEMBERS - s] = on_by(out[s], -s)


def latitude_weight(offset):
    ratio = offset.astype(F32) * (1.0 / (RAD + 1.0))
    return jnp.where(jnp.abs(offset) <= RAD, (1.0 - ratio * ratio) * (1.0 - ratio * ratio), 0.0)


def transform_kernel(place_ref, recv_ref, anom_ref, out_ref, bank, moved, coeff):
    chips = recv_ref.shape[0]
    tiles = anom_ref.shape[0]
    same, south, north = None, None, None
    for c in range(chips):
        sums = recv_ref[c].astype(F32)
        offset = CORES * (place_ref[0] - c)
        parts = [latitude_weight(offset + d) * sums for d in (0, -1, 1)]
        if c == 0:
            same, south, north = parts
        else:
            same, south, north = same + parts[0], south + parts[1], north + parts[2]
    lower = lanes_of(same.shape) % POINTS < HALF
    local = same + jnp.where(
        lower, pltpu.roll(south, LANES - HALF, 1), pltpu.roll(north, HALF, 1)
    )
    diag = [local[s * tiles : (s + 1) * tiles] for s in range(ROWS)]
    innov = diag[DIAGS]
    diag[0] = diag[0] + (MEMBERS - 1.0)
    gram, root, inv_root, corr = bank.at[0], bank.at[1], bank.at[2], bank.at[3]
    other_root, other_inv = bank.at[4], bank.at[5]
    square = None
    for s in range(DIAGS):
        part = diag[s] * diag[s]
        if 0 < s < DIAGS - 1:
            part = part + part
        square = part if square is None else square + part
    square = jnp.broadcast_to(jnp.sum(square, axis=0, keepdims=True), square.shape)
    frob = jnp.sqrt(sum_over_groups(square, POINTS))
    inv_frob = 1.0 / frob
    for s in range(DIAGS):
        gram[s] = diag[s] * inv_frob
    mirror(gram)
    for s in range(MEMBERS):
        inv_root[s] = -0.5 * gram[s] + (1.5 if s == 0 else 0.0)
    product(gram, inv_root, root)
    for sweep in range(1, NS_ITERS):
        product(inv_root, root, corr, -0.5, 1.5)
        if sweep < NS_ITERS - 1:
            product(root, corr, other_root)
        product(corr, inv_root, other_inv)
        root, other_root = other_root, root
        inv_root, other_inv = other_inv, inv_root
    half = shifted_sum(lambda t: inv_root[(-t) % MEMBERS] * innov)
    mean_weights = shifted_sum(lambda t: inv_root[(-t) % MEMBERS] * half) * inv_frob
    factor = math.sqrt(MEMBERS - 1.0) / jnp.sqrt(frob)
    for s in range(MEMBERS):
        value = inv_root[s] * factor + on_by(mean_weights, s)
        coeff[pl.ds(s * tiles, tiles), :] = value.astype(BF16).astype(F32)
    for k in range(tiles):
        moved[0, k] = anom_ref[k].astype(BF16).astype(F32)
    for t in range(1, GROUP):
        for k in range(tiles):
            moved[t, k] = shifted_tile(lambda j: moved[0, j % tiles], k, t, POINTS)
    for k in range(tiles):
        mixed = None
        for s in range(MEMBERS):
            on, t = divmod(s, GROUP)
            part = moved[t, (k + on) % tiles] * coeff[pl.ds(s * tiles + k, 1), :]
            mixed = part if mixed is None else mixed + part
        mixed = mixed - anom_ref[k]
        low = mixed[:HROWS]
        high = jnp.concatenate([mixed[HROWS:], jnp.zeros((2 * HROWS - VROWS, LANES), F32)], axis=0)
        first = lanes_of(low.shape) % POINTS < HALF
        out_ref[CORES * k] = jnp.where(first, low, pltpu.roll(high, HALF, 1)).astype(BF16)
        out_ref[CORES * k + 1] = jnp.where(first, pltpu.roll(low, LANES - HALF, 1), high).astype(BF16)


def transform(place, recv, anomaly):
    tiles = anomaly.shape[0]
    full = pl.BlockSpec(memory_space=pltpu.VMEM)
    return pl.pallas_call(
        transform_kernel,
        in_specs=[pl.BlockSpec(memory_space=pltpu.SMEM), full, full],
        out_specs=full,
        out_shape=jax.ShapeDtypeStruct((CORES * tiles, HROWS, LANES), BF16),
        scratch_shapes=[
            pltpu.VMEM((6, MEMBERS, tiles, LANES), F32),
            pltpu.VMEM((GROUP, tiles, VROWS, LANES), F32),
            pltpu.VMEM((MEMBERS * tiles, LANES), F32),
        ],
        compiler_params=SMALL,
        name="transform",
    )(place, recv, anomaly)


def strips_kernel(recv_ref, out_ref):
    halves = recv_ref.shape[0]
    variables = out_ref.shape[1]
    per = LANES // HALF
    parts = [recv_ref[h].astype(F32) for h in range(halves)]
    group = lax.rem(lanes_of(parts[0].shape) + (LANES - HALO), LANES) // HALF
    first = lanes_of(parts[0].shape) < HALO
    for m in range(GROUP):
        for side in range(2):
            tiles = []
            for c in range(halves // per):
                tile = None
                for j in range(per):
                    piece = parts[per * c + j]
                    move = (HALF * (j - side) - POINTS * m + HALO) % LANES
                    if move:
                        piece = pltpu.roll(piece, move, 1)
                    tile = piece if tile is None else jnp.where(group == j, piece, tile)
                tiles.append(tile)
            for c in range(len(tiles)):
                tile = jnp.where(first, tiles[c - 1], tiles[c])
                at = pl.ds(c * LANES, LANES)
                if side == 0:
                    out_ref[m, 0:HROWS, 0, at] = tile
                else:
                    out_ref[m, HROWS:variables, 0, at] = tile[: variables - HROWS]


def strips(recv, variables):
    halves = recv.shape[0]
    full = pl.BlockSpec(memory_space=pltpu.VMEM)
    return pl.pallas_call(
        strips_kernel,
        in_specs=[full],
        out_specs=full,
        out_shape=jax.ShapeDtypeStruct((GROUP, variables, 1, halves * HALF), F32),
        compiler_params=SMALL,
        name="strips",
    )(recv)


def body(hidden_in, norm_gain, w_in, w_out, w_dec, observed, obs_count, obs_error):
    mem_dev, tok_dev, width = hidden_in.shape
    variables, lon_dev, lat_all = observed.shape
    n_mem, n_tile = lax.axis_size("mem"), lax.axis_size("tile")
    chips = n_tile // CORES
    mem, tile = lax.axis_index("mem"), lax.axis_index("tile")
    chip_place = lax.div(tile, CORES).astype(jnp.int32).reshape(1)
    place = lax.axis_index(("mem", "tile")).astype(jnp.int32).reshape(1)
    n_y = n_mem // 2
    by_chip = [
        [m * n_tile + c * CORES + k for m in range(n_mem) for k in range(CORES)] for c in range(chips)
    ]
    by_core = [[c * CORES + k for c in range(chips)] for k in range(CORES)]

    fields, *seen = forecast(
        place,
        n_y,
        hidden_in.reshape(mem_dev * tok_dev, width),
        norm_gain,
        w_in,
        w_out,
        w_dec,
        jnp.transpose(observed, (1, 2, 0)),
        jnp.transpose(obs_count, (1, 2, 0)),
    )
    halves = lax.all_to_all(
        fields, ("mem", "tile"), 0, 0, tiled=True, axis_index_groups=by_chip
    )

    mems, tiles = np.divmod(np.arange(n_mem * n_tile), n_tile)
    obs = []
    for k, move in enumerate(SENDS):
        targets = []
        for m, t in zip(mems.tolist(), tiles.tolist()):
            half, chip = served_here(m, t, move, (n_tile, n_y))
            targets.append((m * n_tile + t, half // CORES * n_tile + CORES * chip + half % CORES))
        obs.append(lax.ppermute(seen[k], ("mem", "tile"), targets))

    sums, weighted, mean, anomaly = pairs(halves, obs_error)
    smoothed = smooth(sums, weighted, mean, obs, chips)
    rows = lax.all_to_all(smoothed, "tile", 0, 0, tiled=True, axis_index_groups=by_core)
    increments = transform(chip_place, rows, anomaly)
    back = lax.all_to_all(
        increments, ("mem", "tile"), 0, 0, tiled=True, axis_index_groups=by_chip
    )
    return strips(back, variables)


def solution(mesh):
    return jax.shard_map(
        body,
        mesh=mesh,
        in_specs=(
            P("mem", "tile", None),
            P(),
            P(),
            P(),
            P(),
            P(None, "tile", None),
            P(None, "tile", None),
            P(),
        ),
        out_specs=P("mem", None, "tile", None),
        check_vma=False,
    )
```

```python
import functools
import math

import jax
import jax.numpy as jnp
import numpy as np
from jax import lax
from jax.experimental import pallas as pl
from jax.experimental.pallas import tpu as pltpu
from jax.sharding import PartitionSpec as P

RAD = 6
NS_ITERS = 4
F32 = jnp.float32
BF16 = jnp.bfloat16

LANES = 128
VROWS = 72
HROWS = 40
CORES = 2
HALF = 16
HALO = 8
WINDOW = HALF + 2 * HALO
POINTS = CORES * HALF
MEMBERS = 32
GROUP = 4
DIAGS = MEMBERS // 2 + 1
ROWS = DIAGS + 1
FF_BLOCK = 1024
TOKEN_BLOCK = 512

UNSEEN = 1e30
COUNT = 3.0

LARGE = pltpu.CompilerParams(vmem_limit_bytes=60 * 2**20)
SMALL = pltpu.CompilerParams(vmem_limit_bytes=12 * 2**20)


def lanes_of(shape):
    return lax.broadcasted_iota(jnp.int32, shape, len(shape) - 1)


def gelu(h):
    inner = h * (math.sqrt(2.0 / math.pi) + (0.044715 * math.sqrt(2.0 / math.pi)) * (h * h))
    half = 0.5 * h
    return half + half * jnp.tanh(inner)


SENDS = (0, -1)


def served(mem, tile, move, ways):
    n_tile, n_y = ways
    half = lax.rem(tile + (n_tile + move), n_tile)
    to_mem = lax.div(half, CORES)
    z_lo, y = lax.div(mem, n_y), lax.rem(mem, n_y)
    to_z_lo, to_y = lax.div(to_mem, n_y), lax.rem(to_mem, n_y)
    chip = lax.div(tile, CORES)
    x, z_hi = lax.div(chip, 2), lax.rem(chip, 2)
    n_x = n_tile // (2 * CORES)
    to_x = lax.rem(x + 2 + to_y - y + 2 * n_x, n_x)
    to_z_hi = lax.rem(z_hi + z_lo + to_z_lo, 2)
    return half, 2 * to_x + to_z_hi


def served_here(mem, tile, move, ways):
    n_tile, n_y = ways
    half = (tile + n_tile + move) % n_tile
    to_mem = half // CORES
    z_lo, y = mem // n_y, mem % n_y
    to_z_lo, to_y = to_mem // n_y, to_mem % n_y
    chip = tile // CORES
    x, z_hi = chip // 2, chip % 2
    n_x = n_tile // (2 * CORES)
    to_x = (x + 2 + to_y - y) % n_x
    to_z_hi = (z_hi + z_lo + to_z_lo) % 2
    return half, 2 * to_x + to_z_hi


def forecast_kernel(
    place_ref, x_ref, gain_ref, win_ref, wout_ref, wdec_ref, obs_ref, count_ref, out_ref, west_ref, east_ref,
    normed, acc, decoder, *, n_y,
):
    step = pl.program_id(0)
    steps = pl.num_programs(0)
    tokens = x_ref.shape[0]
    blocks = tokens // TOKEN_BLOCK
    lon_all = tokens // GROUP

    @pl.when(step == 0)
    def _():
        gain = gain_ref[...].astype(F32).reshape(1, -1)
        n_tile = out_ref.shape[0]
        mem, tile = lax.div(place_ref[0], n_tile), lax.rem(place_ref[0], n_tile)
        for seen_ref, move in zip((west_ref, east_ref), SENDS):
            _, chip = served(mem, tile, move, (n_tile, n_y))
            for r in range(CORES):
                row = CORES * chip + r
                seen_ref[r] = jnp.where(count_ref[:, row, :] > 0, obs_ref[:, row, :], UNSEEN)
        decoder[...] = jnp.zeros_like(decoder)
        decoder[0 : wdec_ref.shape[0], :] = wdec_ref[...]
        for r in range(tokens // 128):
            xf = x_ref[pl.ds(r * 128, 128), :].astype(F32)
            centred = xf - jnp.mean(xf, axis=-1, keepdims=True)
            spread = jnp.mean(centred * centred, axis=-1, keepdims=True)
            normed[pl.ds(r * 128, 128), :] = (centred * lax.rsqrt(spread + 1e-05) * gain).astype(BF16)

    def up(r):
        return jnp.dot(
            normed[pl.ds(r * TOKEN_BLOCK, TOKEN_BLOCK), :], win_ref[...], preferred_element_type=F32
        )

    def run(first):
        hidden = up(0)
        for r in range(blocks):
            following = up(r + 1) if r + 1 < blocks else None
            down = jnp.dot(gelu(hidden).astype(BF16), wout_ref[...], preferred_element_type=F32)
            at = pl.ds(r * TOKEN_BLOCK, TOKEN_BLOCK)
            if first:
                acc[at, :] = down
            else:
                acc[at, :] += down
            hidden = following

    @pl.when(step == 0)
    def _():
        run(True)

    @pl.when(step > 0)
    def _():
        run(False)

    @pl.when(step == steps - 1)
    def _():
        wdec = decoder[...]
        contract = (((1,), (1,)), ((), ()))
        for r in range(blocks):
            at = pl.ds(r * TOKEN_BLOCK, TOKEN_BLOCK)
            layer_out = (x_ref[at, :].astype(F32) + acc[at, :]).astype(BF16)
            fields = lax.dot_general(layer_out, wdec, contract, preferred_element_type=F32)
            acc[at, 0 : 2 * HROWS] = fields
        for h in range(lon_all // HALF):
            window = []
            for m in range(GROUP):
                for at in (HALF * h, HALF * (h + 1)):
                    window.append(acc[pl.ds(m * lon_all + at % lon_all, HALF), 0:LANES])
            out_ref[h] = jnp.concatenate(window, axis=0).T[:VROWS].astype(BF16)


def forecast(place, n_y, x, gain, w_in, w_out, w_dec, observed, obs_count):
    tokens, width = x.shape
    hidden = w_in.shape[1]
    halves = tokens // GROUP // HALF
    lon_dev, _, variables = observed.shape
    whole = pl.BlockSpec(observed.shape, lambda s: (0, 0, 0))
    return pl.pallas_call(
        functools.partial(forecast_kernel, n_y=n_y),
        grid=(hidden // FF_BLOCK,),
        in_specs=[
            pl.BlockSpec(memory_space=pltpu.SMEM),
            pl.BlockSpec((tokens, width), lambda s: (0, 0)),
            pl.BlockSpec((width,), lambda s: (0,)),
            pl.BlockSpec((width, FF_BLOCK), lambda s: (0, s)),
            pl.BlockSpec((FF_BLOCK, width), lambda s: (s, 0)),
            pl.BlockSpec(w_dec.shape, lambda s: (0, 0)),
            whole,
            whole,
        ],
        out_specs=(
            pl.BlockSpec((halves, VROWS, LANES), lambda s: (0, 0, 0)),
            pl.BlockSpec((CORES, lon_dev, variables), lambda s: (0, 0, 0)),
            pl.BlockSpec((CORES, lon_dev, variables), lambda s: (0, 0, 0)),
        ),
        out_shape=(
            jax.ShapeDtypeStruct((halves, VROWS, LANES), BF16),
            jax.ShapeDtypeStruct((CORES, lon_dev, variables), F32),
            jax.ShapeDtypeStruct((CORES, lon_dev, variables), F32),
        ),
        scratch_shapes=[
            pltpu.VMEM((tokens, width), BF16),
            pltpu.VMEM((tokens, width), F32),
            pltpu.VMEM((2 * HROWS, width), BF16),
        ],
        compiler_params=LARGE,
        cost_estimate=pl.CostEstimate(
            flops=4 * tokens * width * hidden, bytes_accessed=4 * width * hidden, transcendentals=0
        ),
        name="forecast",
    )(place, x, gain, w_in, w_out, w_dec, observed, obs_count)


def sum_over_groups(tile, width):
    while width < LANES:
        tile = tile + pltpu.roll(tile, width, 1)
        width *= 2
    return tile


def shifted_tile(tiles, index, shift, width):
    move = shift * width
    if not move:
        return tiles(index)
    here = pltpu.roll(tiles(index), LANES - move, 1)
    there = pltpu.roll(tiles(index + 1), LANES - move, 1)
    return jnp.where(lanes_of(here.shape) < LANES - move, here, there)


def pair_sums(fields, prec, width, weighted, moved, put):
    count = len(fields)
    per = LANES // width
    total = fields[0]
    for tile in fields[1:]:
        total = total + tile
    mean = sum_over_groups(total, width) / MEMBERS
    anomalies = []
    for k in range(count):
        anomaly = fields[k] - mean
        anomalies.append(anomaly)
        weighted[k] = (anomaly * prec).astype(BF16).astype(F32)
        moved[0, k] = anomaly.astype(BF16).astype(F32)
    for t in range(1, per):
        for k in range(count):
            moved[t, k] = shifted_tile(lambda j: moved[0, j % count], k, t, width)
    for s in range(DIAGS):
        on, t = divmod(s, per)
        for k in range(count):
            put(s, k, jnp.sum(weighted[k] * moved[t, (k + on) % count], axis=0, keepdims=True))
    return mean, anomalies


def pairs_kernel(recv_ref, err_ref, sums, weighted, mean_ref, anom_ref, wide, moved):
    tiles = recv_ref.shape[0] // CORES
    variables = err_ref.shape[0]
    wide[...] = jnp.zeros_like(wide)
    wide[0:1, 0:variables] = err_ref[...].reshape(1, variables)
    err = jnp.broadcast_to(wide[0:1, :], (LANES, LANES)).T[:VROWS]
    is_variable = lax.broadcasted_iota(jnp.int32, err.shape, 0) < variables
    prec = jnp.where(is_variable, COUNT / (err * err), 0.0)

    sums[pl.ds(DIAGS * tiles, tiles), :] = jnp.zeros((tiles, CORES * LANES), F32)
    anomalies = []
    for r in range(CORES):

        def put(s, k, row):
            sums[pl.ds(s * tiles + k, 1), r * LANES : (r + 1) * LANES] = row

        fields = [recv_ref[CORES * m + r].astype(F32) for m in range(tiles)]
        mean, anomaly = pair_sums(fields, prec, WINDOW, weighted.at[r], moved.at[r], put)
        mean_ref[r] = mean
        anomalies.append(anomaly)
    lower = lanes_of((VROWS, LANES)) % POINTS < HALF
    for k in range(tiles):
        anom_ref[k] = jnp.where(
            lower,
            pltpu.roll(anomalies[0][k], LANES - HALO, 1),
            pltpu.roll(anomalies[1][k], HALF - HALO, 1),
        )


def smooth_kernel(sums_ref, weighted, mean_ref, west_ref, east_ref, taper_ref, out_ref, wide, sums):
    tiles = weighted.shape[1]
    variables = west_ref.shape[2]
    wide[...] = jnp.zeros_like(wide)
    for r in range(CORES):
        at = slice(r * LANES, (r + 1) * LANES)
        wide[0:HALF, 0:variables] = west_ref[r]
        wide[HALF:WINDOW, 0:variables] = east_ref[r]
        obs = jnp.concatenate([wide[...]] * GROUP, axis=0).T[:VROWS]
        is_seen = obs[0:1] < 0.5 * UNSEEN
        innovation = obs - mean_ref[r]
        diags = sums_ref[0 : DIAGS * tiles, at]
        sums[0 : DIAGS * tiles, at] = jnp.where(is_seen, diags, 0.0)
        for k in range(tiles):
            row = jnp.sum(weighted[r, k] * innovation, axis=0, keepdims=True)
            sums[pl.ds(DIAGS * tiles + k, 1), at] = jnp.where(is_seen, row, 0.0)
    smooth = jnp.dot(
        sums[...], taper_ref[...], precision=lax.Precision.HIGHEST, preferred_element_type=F32
    ).astype(BF16)
    for c in range(out_ref.shape[0]):
        out_ref[c] = smooth


def taper_of(offset):
    offset = np.asarray(offset, np.float32)
    ratio = offset / np.float32(RAD + 1.0)
    return np.where(np.abs(offset) <= RAD, (1.0 - ratio * ratio) ** 2, 0.0).astype(np.float32)


def longitude_taper():
    lat, rest = np.divmod(np.arange(CORES * LANES), LANES)
    member, col = np.divmod(rest, WINDOW)
    out_member, rest = np.divmod(np.arange(LANES), POINTS)
    out_lat, out_col = np.divmod(rest, HALF)
    same = (lat[:, None] == out_lat[None, :]) & (member[:, None] == out_member[None, :])
    weight = taper_of(col[:, None] - HALO - out_col[None, :])
    return jnp.asarray(np.where(same, weight, 0.0).astype(np.float32))


def pairs(recv, err):
    tiles = recv.shape[0] // CORES
    full = pl.BlockSpec(memory_space=pltpu.VMEM)
    return pl.pallas_call(
        pairs_kernel,
        in_specs=[full] * 2,
        out_specs=(full,) * 4,
        out_shape=(
            jax.ShapeDtypeStruct((ROWS * tiles, CORES * LANES), F32),
            jax.ShapeDtypeStruct((CORES, tiles, VROWS, LANES), F32),
            jax.ShapeDtypeStruct((CORES, VROWS, LANES), F32),
            jax.ShapeDtypeStruct((tiles, VROWS, LANES), F32),
        ),
        scratch_shapes=[
            pltpu.VMEM((8, LANES), F32),
            pltpu.VMEM((CORES, LANES // WINDOW, tiles, VROWS, LANES), F32),
        ],
        compiler_params=SMALL,
        name="pairs",
    )(recv, err)


def smooth(sums, weighted, mean, obs, chips):
    full = pl.BlockSpec(memory_space=pltpu.VMEM)
    return pl.pallas_call(
        smooth_kernel,
        in_specs=[full] * 6,
        out_specs=full,
        out_shape=jax.ShapeDtypeStruct((chips, sums.shape[0], LANES), BF16),
        scratch_shapes=[pltpu.VMEM((WINDOW, LANES), F32), pltpu.VMEM(sums.shape, F32)],
        compiler_params=SMALL,
        name="smooth",
    )(sums, weighted, mean, *obs, longitude_taper())


def on_by(x, n):
    sub, t = divmod(n % MEMBERS, GROUP)
    if t:
        move = LANES - POINTS * t
        x = pltpu.roll(x, move, 1)
        x = jnp.where(lanes_of(x.shape) < move, x, pltpu.roll(x, 7, 0))
    if sub:
        x = pltpu.roll(x, 8 - sub, 0)
    return x


def shifted_sum(term):
    total = None
    for t in range(GROUP - 1, -1, -1):
        inner = None
        for a in range(MEMBERS // GROUP - 1, -1, -1):
            part = term(GROUP * a + t)
            inner = part if inner is None else on_by(inner, GROUP) + part
        total = inner if total is None else on_by(total, 1) + inner
    return total


def spread(right, turned):
    for u in range(MEMBERS):
        value = right[u]
        for a in range(MEMBERS // GROUP):
            turned[a, u] = on_by(value, GROUP * a)


def product(left, turned, out, scale=None, shift=None):
    moved = [on_by(left[(-t) % MEMBERS], t // GROUP * GROUP) for t in range(MEMBERS)]
    for s in range(DIAGS):
        value = None
        for t in range(GROUP - 1, -1, -1):
            parts = [
                moved[at] * turned[at // GROUP, (s - at) % MEMBERS] for at in range(t, MEMBERS, GROUP)
            ]
            while len(parts) > 1:
                parts = [a + b for a, b in zip(parts[::2], parts[1::2])]
            value = parts[0] if value is None else on_by(value, 1) + parts[0]
        if scale is not None:
            value = scale * value
            if s == 0:
                value = value + shift
        out[s] = value
    mirror(out)


def mirror(out):
    for s in range(1, MEMBERS - DIAGS + 1):
        out[MEMBERS - s] = on_by(out[s], -s)


def latitude_weight(offset):
    ratio = offset.astype(F32) * (1.0 / (RAD + 1.0))
    return jnp.where(jnp.abs(offset) <= RAD, (1.0 - ratio * ratio) * (1.0 - ratio * ratio), 0.0)


def transform_kernel(place_ref, recv_ref, anom_ref, out_ref, bank, turned, moved, coeff):
    chips = recv_ref.shape[0]
    tiles = anom_ref.shape[0]
    same, south, north = None, None, None
    for c in range(chips):
        sums = recv_ref[c].astype(F32)
        offset = CORES * (place_ref[0] - c)
        parts = [latitude_weight(offset + d) * sums for d in (0, -1, 1)]
        if c == 0:
            same, south, north = parts
        else:
            same, south, north = same + parts[0], south + parts[1], north + parts[2]
    lower = lanes_of(same.shape) % POINTS < HALF
    local = same + jnp.where(
        lower, pltpu.roll(south, LANES - HALF, 1), pltpu.roll(north, HALF, 1)
    )
    diag = [local[s * tiles : (s + 1) * tiles] for s in range(ROWS)]
    innov = diag[DIAGS]
    diag[0] = diag[0] + (MEMBERS - 1.0)
    gram, root, inv_root, corr = bank.at[0], bank.at[1], bank.at[2], bank.at[3]
    other_root, other_inv = bank.at[4], bank.at[5]
    square = None
    for s in range(DIAGS):
        part = diag[s] * diag[s]
        if 0 < s < DIAGS - 1:
            part = part + part
        square = part if square is None else square + part
    square = jnp.broadcast_to(jnp.sum(square, axis=0, keepdims=True), square.shape)
    frob = jnp.sqrt(sum_over_groups(square, POINTS))
    inv_frob = 1.0 / frob
    for s in range(DIAGS):
        gram[s] = diag[s] * inv_frob
    mirror(gram)
    for s in range(MEMBERS):
        inv_root[s] = -0.5 * gram[s] + (1.5 if s == 0 else 0.0)
    spread(inv_root, turned)
    product(gram, turned, root)
    for sweep in range(1, NS_ITERS):
        spread(root, turned)
        product(inv_root, turned, corr, -0.5, 1.5)
        spread(corr, turned)
        if sweep < NS_ITERS - 1:
            product(root, turned, other_root)
        product(inv_root, turned, other_inv)
        root, other_root = other_root, root
        inv_root, other_inv = other_inv, inv_root
    half = shifted_sum(lambda t: inv_root[(-t) % MEMBERS] * innov)
    mean_weights = shifted_sum(lambda t: inv_root[(-t) % MEMBERS] * half) * inv_frob
    factor = math.sqrt(MEMBERS - 1.0) / jnp.sqrt(frob)
    for s in range(MEMBERS):
        value = inv_root[s] * factor + on_by(mean_weights, s)
        coeff[pl.ds(s * tiles, tiles), :] = value.astype(BF16).astype(F32)
    for k in range(tiles):
        moved[0, k] = anom_ref[k].astype(BF16).astype(F32)
    for t in range(1, GROUP):
        for k in range(tiles):
            moved[t, k] = shifted_tile(lambda j: moved[0, j % tiles], k, t, POINTS)
    for k in range(tiles):
        mixed = -anom_ref[k]
        for on in range(tiles):
            parts = [
                moved[t, (k + on) % tiles] * coeff[pl.ds((GROUP * on + t) * tiles + k, 1), :]
                for t in range(GROUP)
            ]
            mixed = mixed + ((parts[0] + parts[1]) + (parts[2] + parts[3]))
        low = mixed[:HROWS]
        high = jnp.concatenate([mixed[HROWS:], jnp.zeros((2 * HROWS - VROWS, LANES), F32)], axis=0)
        first = lanes_of(low.shape) % POINTS < HALF
        out_ref[CORES * k] = jnp.where(first, low, pltpu.roll(high, HALF, 1)).astype(BF16)
        out_ref[CORES * k + 1] = jnp.where(first, pltpu.roll(low, LANES - HALF, 1), high).astype(BF16)


def transform(place, recv, anomaly):
    tiles = anomaly.shape[0]
    full = pl.BlockSpec(memory_space=pltpu.VMEM)
    return pl.pallas_call(
        transform_kernel,
        in_specs=[pl.BlockSpec(memory_space=pltpu.SMEM), full, full],
        out_specs=full,
        out_shape=jax.ShapeDtypeStruct((CORES * tiles, HROWS, LANES), BF16),
        scratch_shapes=[
            pltpu.VMEM((6, MEMBERS, tiles, LANES), F32),
            pltpu.VMEM((MEMBERS // GROUP, MEMBERS, tiles, LANES), F32),
            pltpu.VMEM((GROUP, tiles, VROWS, LANES), F32),
            pltpu.VMEM((MEMBERS * tiles, LANES), F32),
        ],
        compiler_params=SMALL,
        name="transform",
    )(place, recv, anomaly)


def strips_kernel(recv_ref, out_ref):
    halves = recv_ref.shape[0]
    variables = out_ref.shape[1]
    per = LANES // HALF
    parts = [recv_ref[h].astype(F32) for h in range(halves)]
    group = lax.rem(lanes_of(parts[0].shape) + (LANES - HALO), LANES) // HALF
    first = lanes_of(parts[0].shape) < HALO
    for m in range(GROUP):
        for side in range(2):
            tiles = []
            for c in range(halves // per):
                tile = None
                for j in range(per):
                    piece = parts[per * c + j]
                    move = (HALF * (j - side) - POINTS * m + HALO) % LANES
                    if move:
                        piece = pltpu.roll(piece, move, 1)
                    tile = piece if tile is None else jnp.where(group == j, piece, tile)
                tiles.append(tile)
            for c in range(len(tiles)):
                tile = jnp.where(first, tiles[c - 1], tiles[c])
                at = pl.ds(c * LANES, LANES)
                if side == 0:
                    out_ref[m, 0:HROWS, 0, at] = tile
                else:
                    out_ref[m, HROWS:variables, 0, at] = tile[: variables - HROWS]


def strips(recv, variables):
    halves = recv.shape[0]
    full = pl.BlockSpec(memory_space=pltpu.VMEM)
    return pl.pallas_call(
        strips_kernel,
        in_specs=[full],
        out_specs=full,
        out_shape=jax.ShapeDtypeStruct((GROUP, variables, 1, halves * HALF), F32),
        compiler_params=SMALL,
        name="strips",
    )(recv)


def body(hidden_in, norm_gain, w_in, w_out, w_dec, observed, obs_count, obs_error):
    mem_dev, tok_dev, width = hidden_in.shape
    variables, lon_dev, lat_all = observed.shape
    n_mem, n_tile = lax.axis_size("mem"), lax.axis_size("tile")
    chips = n_tile // CORES
    mem, tile = lax.axis_index("mem"), lax.axis_index("tile")
    chip_place = lax.div(tile, CORES).astype(jnp.int32).reshape(1)
    place = lax.axis_index(("mem", "tile")).astype(jnp.int32).reshape(1)
    n_y = n_mem // 2
    by_chip = [
        [m * n_tile + c * CORES + k for m in range(n_mem) for k in range(CORES)] for c in range(chips)
    ]
    by_core = [[c * CORES + k for c in range(chips)] for k in range(CORES)]

    fields, *seen = forecast(
        place,
        n_y,
        hidden_in.reshape(mem_dev * tok_dev, width),
        norm_gain,
        w_in,
        w_out,
        w_dec,
        jnp.transpose(observed, (1, 2, 0)),
        jnp.transpose(obs_count, (1, 2, 0)),
    )
    halves = lax.all_to_all(
        fields, ("mem", "tile"), 0, 0, tiled=True, axis_index_groups=by_chip
    )

    mems, tiles = np.divmod(np.arange(n_mem * n_tile), n_tile)
    obs = []
    for k, move in enumerate(SENDS):
        targets = []
        for m, t in zip(mems.tolist(), tiles.tolist()):
            half, chip = served_here(m, t, move, (n_tile, n_y))
            targets.append((m * n_tile + t, half // CORES * n_tile + CORES * chip + half % CORES))
        obs.append(lax.ppermute(seen[k], ("mem", "tile"), targets))

    sums, weighted, mean, anomaly = pairs(halves, obs_error)
    smoothed = smooth(sums, weighted, mean, obs, chips)
    rows = lax.all_to_all(smoothed, "tile", 0, 0, tiled=True, axis_index_groups=by_core)
    increments = transform(chip_place, rows, anomaly)
    back = lax.all_to_all(
        increments, ("mem", "tile"), 0, 0, tiled=True, axis_index_groups=by_chip
    )
    return strips(back, variables)


def solution(mesh):
    return jax.shard_map(
        body,
        mesh=mesh,
        in_specs=(
            P("mem", "tile", None),
            P(),
            P(),
            P(),
            P(),
            P(None, "tile", None),
            P(None, "tile", None),
            P(),
        ),
        out_specs=P("mem", None, "tile", None),
        check_vma=False,
    )
```

```python
import functools
import math

import jax
import jax.numpy as jnp
import numpy as np
from jax import lax
from jax.experimental import pallas as pl
from jax.experimental.pallas import tpu as pltpu
from jax.sharding import PartitionSpec as P

RAD = 6
NS_ITERS = 4
F32 = jnp.float32
BF16 = jnp.bfloat16

LANES = 128
VROWS = 72
HROWS = 40
CORES = 2
HALF = 16
HALO = 8
WINDOW = HALF + 2 * HALO
POINTS = CORES * HALF
MEMBERS = 32
GROUP = 4
DIAGS = MEMBERS // 2 + 1
ROWS = DIAGS + 1
FF_BLOCK = 1024
TOKEN_BLOCK = 512

UNSEEN = 1e30
COUNT = 3.0

LARGE = pltpu.CompilerParams(vmem_limit_bytes=60 * 2**20)
SMALL = pltpu.CompilerParams(vmem_limit_bytes=12 * 2**20)


def lanes_of(shape):
    return lax.broadcasted_iota(jnp.int32, shape, len(shape) - 1)


def gelu(h):
    inner = h * (math.sqrt(2.0 / math.pi) + (0.044715 * math.sqrt(2.0 / math.pi)) * (h * h))
    half = 0.5 * h
    return half + half * jnp.tanh(inner)


SENDS = (0, -1)


def served(mem, tile, move, ways):
    n_tile, n_y = ways
    half = lax.rem(tile + (n_tile + move), n_tile)
    to_mem = lax.div(half, CORES)
    z_lo, y = lax.div(mem, n_y), lax.rem(mem, n_y)
    to_z_lo, to_y = lax.div(to_mem, n_y), lax.rem(to_mem, n_y)
    chip = lax.div(tile, CORES)
    x, z_hi = lax.div(chip, 2), lax.rem(chip, 2)
    n_x = n_tile // (2 * CORES)
    to_x = lax.rem(x + 2 + to_y - y + 2 * n_x, n_x)
    to_z_hi = lax.rem(z_hi + z_lo + to_z_lo, 2)
    return half, 2 * to_x + to_z_hi


def served_here(mem, tile, move, ways):
    n_tile, n_y = ways
    half = (tile + n_tile + move) % n_tile
    to_mem = half // CORES
    z_lo, y = mem // n_y, mem % n_y
    to_z_lo, to_y = to_mem // n_y, to_mem % n_y
    chip = tile // CORES
    x, z_hi = chip // 2, chip % 2
    n_x = n_tile // (2 * CORES)
    to_x = (x + 2 + to_y - y) % n_x
    to_z_hi = (z_hi + z_lo + to_z_lo) % 2
    return half, 2 * to_x + to_z_hi


def forecast_kernel(
    place_ref, x_ref, gain_ref, win_ref, wout_ref, wdec_ref, obs_ref, count_ref, out_ref, west_ref, east_ref,
    normed, acc, decoder, *, n_y,
):
    step = pl.program_id(0)
    steps = pl.num_programs(0)
    tokens = x_ref.shape[0]
    blocks = tokens // TOKEN_BLOCK
    lon_all = tokens // GROUP

    @pl.when(step == 0)
    def _():
        gain = gain_ref[...].astype(F32).reshape(1, -1)
        n_tile = out_ref.shape[0]
        mem, tile = lax.div(place_ref[0], n_tile), lax.rem(place_ref[0], n_tile)
        for seen_ref, move in zip((west_ref, east_ref), SENDS):
            _, chip = served(mem, tile, move, (n_tile, n_y))
            for r in range(CORES):
                row = CORES * chip + r
                seen_ref[r] = jnp.where(count_ref[:, row, :] > 0, obs_ref[:, row, :], UNSEEN)
        decoder[...] = jnp.zeros_like(decoder)
        decoder[0 : wdec_ref.shape[0], :] = wdec_ref[...].astype(F32)
        for r in range(tokens // 128):
            xf = x_ref[pl.ds(r * 128, 128), :].astype(F32)
            centred = xf - jnp.mean(xf, axis=-1, keepdims=True)
            spread = jnp.mean(centred * centred, axis=-1, keepdims=True)
            normed[pl.ds(r * 128, 128), :] = (centred * lax.rsqrt(spread + 1e-05) * gain).astype(BF16)

    def up(r):
        return jnp.dot(
            normed[pl.ds(r * TOKEN_BLOCK, TOKEN_BLOCK), :], win_ref[...], preferred_element_type=F32
        )

    def run(first):
        hidden = up(0)
        for r in range(blocks):
            following = up(r + 1) if r + 1 < blocks else None
            down = jnp.dot(gelu(hidden).astype(BF16), wout_ref[...], preferred_element_type=F32)
            at = pl.ds(r * TOKEN_BLOCK, TOKEN_BLOCK)
            if first:
                acc[at, :] = down
            else:
                acc[at, :] += down
            hidden = following

    @pl.when(step == 0)
    def _():
        run(True)

    @pl.when(step > 0)
    def _():
        run(False)

    @pl.when(step == steps - 1)
    def _():
        wdec = decoder[...].astype(BF16)
        contract = (((1,), (1,)), ((), ()))
        for r in range(blocks):
            at = pl.ds(r * TOKEN_BLOCK, TOKEN_BLOCK)
            layer_out = (x_ref[at, :].astype(F32) + acc[at, :]).astype(BF16)
            fields = lax.dot_general(layer_out, wdec, contract, preferred_element_type=F32)
            acc[at, 0 : 2 * HROWS] = fields
        for h in range(lon_all // HALF):
            window = []
            for m in range(GROUP):
                for at in (HALF * h, HALF * (h + 1)):
                    window.append(acc[pl.ds(m * lon_all + at % lon_all, HALF), 0:LANES])
            out_ref[h] = jnp.concatenate(window, axis=0).T[:VROWS].astype(BF16)


def forecast(place, n_y, x, gain, w_in, w_out, w_dec, observed, obs_count):
    tokens, width = x.shape
    hidden = w_in.shape[1]
    halves = tokens // GROUP // HALF
    lon_dev, _, variables = observed.shape
    whole = pl.BlockSpec(observed.shape, lambda s: (0, 0, 0))
    return pl.pallas_call(
        functools.partial(forecast_kernel, n_y=n_y),
        grid=(hidden // FF_BLOCK,),
        in_specs=[
            pl.BlockSpec(memory_space=pltpu.SMEM),
            pl.BlockSpec((tokens, width), lambda s: (0, 0)),
            pl.BlockSpec((width,), lambda s: (0,)),
            pl.BlockSpec((width, FF_BLOCK), lambda s: (0, s)),
            pl.BlockSpec((FF_BLOCK, width), lambda s: (s, 0)),
            pl.BlockSpec(w_dec.shape, lambda s: (0, 0)),
            whole,
            whole,
        ],
        out_specs=(
            pl.BlockSpec((halves, VROWS, LANES), lambda s: (0, 0, 0)),
            pl.BlockSpec((CORES, lon_dev, variables), lambda s: (0, 0, 0)),
            pl.BlockSpec((CORES, lon_dev, variables), lambda s: (0, 0, 0)),
        ),
        out_shape=(
            jax.ShapeDtypeStruct((halves, VROWS, LANES), BF16),
            jax.ShapeDtypeStruct((CORES, lon_dev, variables), F32),
            jax.ShapeDtypeStruct((CORES, lon_dev, variables), F32),
        ),
        scratch_shapes=[
            pltpu.VMEM((tokens, width), BF16),
            pltpu.VMEM((tokens, width), F32),
            pltpu.VMEM((2 * HROWS, width), F32),
        ],
        compiler_params=LARGE,
        cost_estimate=pl.CostEstimate(
            flops=4 * tokens * width * hidden, bytes_accessed=4 * width * hidden, transcendentals=0
        ),
        name="forecast",
    )(place, x, gain, w_in, w_out, w_dec, observed, obs_count)


def sum_over_groups(tile, width):
    while width < LANES:
        tile = tile + pltpu.roll(tile, width, 1)
        width *= 2
    return tile


def shifted_tile(tiles, index, shift, width):
    move = shift * width
    if not move:
        return tiles(index)
    here = pltpu.roll(tiles(index), LANES - move, 1)
    there = pltpu.roll(tiles(index + 1), LANES - move, 1)
    return jnp.where(lanes_of(here.shape) < LANES - move, here, there)


def pair_sums(fields, prec, width, weighted, moved, put):
    count = len(fields)
    per = LANES // width
    total = fields[0]
    for tile in fields[1:]:
        total = total + tile
    mean = sum_over_groups(total, width) / MEMBERS
    anomalies = []
    for k in range(count):
        anomaly = fields[k] - mean
        anomalies.append(anomaly)
        weighted[k] = (anomaly * prec).astype(BF16).astype(F32)
        moved[0, k] = anomaly.astype(BF16).astype(F32)
    for t in range(1, per):
        for k in range(count):
            moved[t, k] = shifted_tile(lambda j: moved[0, j % count], k, t, width)
    for s in range(DIAGS):
        on, t = divmod(s, per)
        for k in range(count):
            put(s, k, jnp.sum(weighted[k] * moved[t, (k + on) % count], axis=0, keepdims=True))
    return mean, anomalies


def pairs_kernel(recv_ref, err_ref, sums, weighted, mean_ref, anom_ref, wide, moved):
    tiles = recv_ref.shape[0] // CORES
    variables = err_ref.shape[0]
    wide[...] = jnp.zeros_like(wide)
    wide[0:1, 0:variables] = err_ref[...].reshape(1, variables)
    err = jnp.broadcast_to(wide[0:1, :], (LANES, LANES)).T[:VROWS]
    is_variable = lax.broadcasted_iota(jnp.int32, err.shape, 0) < variables
    prec = jnp.where(is_variable, COUNT / (err * err), 0.0)

    sums[pl.ds(DIAGS * tiles, tiles), :] = jnp.zeros((tiles, CORES * LANES), F32)
    anomalies = []
    for r in range(CORES):

        def put(s, k, row):
            sums[pl.ds(s * tiles + k, 1), r * LANES : (r + 1) * LANES] = row

        fields = [recv_ref[CORES * m + r].astype(F32) for m in range(tiles)]
        mean, anomaly = pair_sums(fields, prec, WINDOW, weighted.at[r], moved.at[r], put)
        mean_ref[r] = mean
        anomalies.append(anomaly)
    lower = lanes_of((VROWS, LANES)) % POINTS < HALF
    for k in range(tiles):
        anom_ref[k] = jnp.where(
            lower,
            pltpu.roll(anomalies[0][k], LANES - HALO, 1),
            pltpu.roll(anomalies[1][k], HALF - HALO, 1),
        )


def smooth_kernel(sums_ref, weighted, mean_ref, west_ref, east_ref, taper_ref, out_ref, wide, sums):
    tiles = weighted.shape[1]
    variables = west_ref.shape[2]
    wide[...] = jnp.zeros_like(wide)
    for r in range(CORES):
        at = slice(r * LANES, (r + 1) * LANES)
        wide[0:HALF, 0:variables] = west_ref[r]
        wide[HALF:WINDOW, 0:variables] = east_ref[r]
        obs = jnp.concatenate([wide[...]] * GROUP, axis=0).T[:VROWS]
        is_seen = obs[0:1] < 0.5 * UNSEEN
        innovation = obs - mean_ref[r]
        diags = sums_ref[0 : DIAGS * tiles, at]
        sums[0 : DIAGS * tiles, at] = jnp.where(is_seen, diags, 0.0)
        for k in range(tiles):
            row = jnp.sum(weighted[r, k] * innovation, axis=0, keepdims=True)
            sums[pl.ds(DIAGS * tiles + k, 1), at] = jnp.where(is_seen, row, 0.0)
    smooth = jnp.dot(
        sums[...], taper_ref[...], precision=lax.Precision.HIGHEST, preferred_element_type=F32
    ).astype(BF16)
    for c in range(out_ref.shape[0]):
        out_ref[c] = smooth


def taper_of(offset):
    offset = np.asarray(offset, np.float32)
    ratio = offset / np.float32(RAD + 1.0)
    return np.where(np.abs(offset) <= RAD, (1.0 - ratio * ratio) ** 2, 0.0).astype(np.float32)


def longitude_taper():
    lat, rest = np.divmod(np.arange(CORES * LANES), LANES)
    member, col = np.divmod(rest, WINDOW)
    out_member, rest = np.divmod(np.arange(LANES), POINTS)
    out_lat, out_col = np.divmod(rest, HALF)
    same = (lat[:, None] == out_lat[None, :]) & (member[:, None] == out_member[None, :])
    weight = taper_of(col[:, None] - HALO - out_col[None, :])
    return jnp.asarray(np.where(same, weight, 0.0).astype(np.float32))


def pairs(recv, err):
    tiles = recv.shape[0] // CORES
    full = pl.BlockSpec(memory_space=pltpu.VMEM)
    return pl.pallas_call(
        pairs_kernel,
        in_specs=[full] * 2,
        out_specs=(full,) * 4,
        out_shape=(
            jax.ShapeDtypeStruct((ROWS * tiles, CORES * LANES), F32),
            jax.ShapeDtypeStruct((CORES, tiles, VROWS, LANES), F32),
            jax.ShapeDtypeStruct((CORES, VROWS, LANES), F32),
            jax.ShapeDtypeStruct((tiles, VROWS, LANES), F32),
        ),
        scratch_shapes=[
            pltpu.VMEM((8, LANES), F32),
            pltpu.VMEM((CORES, LANES // WINDOW, tiles, VROWS, LANES), F32),
        ],
        compiler_params=SMALL,
        name="pairs",
    )(recv, err)


def smooth(sums, weighted, mean, obs, chips):
    full = pl.BlockSpec(memory_space=pltpu.VMEM)
    return pl.pallas_call(
        smooth_kernel,
        in_specs=[full] * 6,
        out_specs=full,
        out_shape=jax.ShapeDtypeStruct((chips, sums.shape[0], LANES), BF16),
        scratch_shapes=[pltpu.VMEM((WINDOW, LANES), F32), pltpu.VMEM(sums.shape, F32)],
        compiler_params=SMALL,
        name="smooth",
    )(sums, weighted, mean, *obs, longitude_taper())


def on_by(x, n):
    sub, t = divmod(n % MEMBERS, GROUP)
    if t:
        move = LANES - POINTS * t
        x = pltpu.roll(x, move, 1)
        x = jnp.where(lanes_of(x.shape) < move, x, pltpu.roll(x, 7, 0))
    if sub:
        x = pltpu.roll(x, 8 - sub, 0)
    return x


def shifted_sum(term):
    total = None
    for t in range(GROUP - 1, -1, -1):
        inner = None
        for a in range(MEMBERS // GROUP - 1, -1, -1):
            part = term(GROUP * a + t)
            inner = part if inner is None else on_by(inner, GROUP) + part
        total = inner if total is None else on_by(total, 1) + inner
    return total


def spread(right, turned):
    for u in range(MEMBERS):
        value = right[u]
        for a in range(MEMBERS // GROUP):
            turned[a, u] = on_by(value, GROUP * a)


def product(left, turned, out, scale=None, shift=None):
    moved = [on_by(left[(-t) % MEMBERS], t // GROUP * GROUP) for t in range(MEMBERS)]
    for s in range(DIAGS):
        value = None
        for t in range(GROUP - 1, -1, -1):
            parts = [
                moved[at] * turned[at // GROUP, (s - at) % MEMBERS] for at in range(t, MEMBERS, GROUP)
            ]
            while len(parts) > 1:
                parts = [a + b for a, b in zip(parts[::2], parts[1::2])]
            value = parts[0] if value is None else on_by(value, 1) + parts[0]
        if scale is not None:
            value = scale * value
            if s == 0:
                value = value + shift
        out[s] = value
    mirror(out)


def mirror(out):
    for s in range(1, MEMBERS - DIAGS + 1):
        out[MEMBERS - s] = on_by(out[s], -s)


def latitude_weight(offset):
    ratio = offset.astype(F32) * (1.0 / (RAD + 1.0))
    return jnp.where(jnp.abs(offset) <= RAD, (1.0 - ratio * ratio) * (1.0 - ratio * ratio), 0.0)


def transform_kernel(place_ref, recv_ref, anom_ref, out_ref, bank, turned, moved, coeff):
    chips = recv_ref.shape[0]
    tiles = anom_ref.shape[0]
    same, south, north = None, None, None
    for c in range(chips):
        sums = recv_ref[c].astype(F32)
        offset = CORES * (place_ref[0] - c)
        parts = [latitude_weight(offset + d) * sums for d in (0, -1, 1)]
        if c == 0:
            same, south, north = parts
        else:
            same, south, north = same + parts[0], south + parts[1], north + parts[2]
    lower = lanes_of(same.shape) % POINTS < HALF
    local = same + jnp.where(
        lower, pltpu.roll(south, LANES - HALF, 1), pltpu.roll(north, HALF, 1)
    )
    diag = [local[s * tiles : (s + 1) * tiles] for s in range(ROWS)]
    innov = diag[DIAGS]
    diag[0] = diag[0] + (MEMBERS - 1.0)
    gram, root, inv_root, corr = bank.at[0], bank.at[1], bank.at[2], bank.at[3]
    other_root, other_inv = bank.at[4], bank.at[5]
    square = None
    for s in range(DIAGS):
        part = diag[s] * diag[s]
        if 0 < s < DIAGS - 1:
            part = part + part
        square = part if square is None else square + part
    square = jnp.broadcast_to(jnp.sum(square, axis=0, keepdims=True), square.shape)
    frob = jnp.sqrt(sum_over_groups(square, POINTS))
    inv_frob = 1.0 / frob
    for s in range(DIAGS):
        gram[s] = diag[s] * inv_frob
    mirror(gram)
    for s in range(MEMBERS):
        inv_root[s] = -0.5 * gram[s] + (1.5 if s == 0 else 0.0)
    spread(inv_root, turned)
    product(gram, turned, root)
    for sweep in range(1, NS_ITERS):
        spread(root, turned)
        product(inv_root, turned, corr, -0.5, 1.5)
        spread(corr, turned)
        if sweep < NS_ITERS - 1:
            product(root, turned, other_root)
        product(inv_root, turned, other_inv)
        root, other_root = other_root, root
        inv_root, other_inv = other_inv, inv_root
    half = shifted_sum(lambda t: inv_root[(-t) % MEMBERS] * innov)
    mean_weights = shifted_sum(lambda t: inv_root[(-t) % MEMBERS] * half) * inv_frob
    factor = math.sqrt(MEMBERS - 1.0) / jnp.sqrt(frob)
    for s in range(MEMBERS):
        value = inv_root[s] * factor + on_by(mean_weights, s)
        coeff[pl.ds(s * tiles, tiles), :] = value.astype(BF16).astype(F32)
    for k in range(tiles):
        moved[0, k] = anom_ref[k].astype(BF16).astype(F32)
    for t in range(1, GROUP):
        for k in range(tiles):
            moved[t, k] = shifted_tile(lambda j: moved[0, j % tiles], k, t, POINTS)
    for k in range(tiles):
        mixed = -anom_ref[k]
        for on in range(tiles):
            parts = [
                moved[t, (k + on) % tiles] * coeff[pl.ds((GROUP * on + t) * tiles + k, 1), :]
                for t in range(GROUP)
            ]
            mixed = mixed + ((parts[0] + parts[1]) + (parts[2] + parts[3]))
        low = mixed[:HROWS]
        high = jnp.concatenate([mixed[HROWS:], jnp.zeros((2 * HROWS - VROWS, LANES), F32)], axis=0)
        first = lanes_of(low.shape) % POINTS < HALF
        out_ref[CORES * k] = jnp.where(first, low, pltpu.roll(high, HALF, 1)).astype(BF16)
        out_ref[CORES * k + 1] = jnp.where(first, pltpu.roll(low, LANES - HALF, 1), high).astype(BF16)


def transform(place, recv, anomaly):
    tiles = anomaly.shape[0]
    full = pl.BlockSpec(memory_space=pltpu.VMEM)
    return pl.pallas_call(
        transform_kernel,
        in_specs=[pl.BlockSpec(memory_space=pltpu.SMEM), full, full],
        out_specs=full,
        out_shape=jax.ShapeDtypeStruct((CORES * tiles, HROWS, LANES), BF16),
        scratch_shapes=[
            pltpu.VMEM((6, MEMBERS, tiles, LANES), F32),
            pltpu.VMEM((MEMBERS // GROUP, MEMBERS, tiles, LANES), F32),
            pltpu.VMEM((GROUP, tiles, VROWS, LANES), F32),
            pltpu.VMEM((MEMBERS * tiles, LANES), F32),
        ],
        compiler_params=SMALL,
        name="transform",
    )(place, recv, anomaly)


def strips_kernel(recv_ref, out_ref):
    halves = recv_ref.shape[0]
    variables = out_ref.shape[1]
    per = LANES // HALF
    parts = [recv_ref[h].astype(F32) for h in range(halves)]
    group = lax.rem(lanes_of(parts[0].shape) + (LANES - HALO), LANES) // HALF
    first = lanes_of(parts[0].shape) < HALO
    held = lanes_of(parts[0].shape) // HALF
    moved = []
    for c in range(halves // per):
        for way in range(per):
            tile = parts[per * c + way]
            for g in range(1, per):
                tile = jnp.where(held == g, parts[per * c + (way + g) % per], tile)
            moved.append(pltpu.roll(tile, (HALF * way + HALO) % LANES, 1))
    for m in range(GROUP):
        for side in range(2):
            tiles = []
            for c in range(halves // per):
                tile = None
                for j in range(per):
                    piece = moved[per * c + (j - 2 * m - side) % per]
                    tile = piece if tile is None else jnp.where(group == j, piece, tile)
                tiles.append(tile)
            for c in range(len(tiles)):
                tile = jnp.where(first, tiles[c - 1], tiles[c])
                at = pl.ds(c * LANES, LANES)
                if side == 0:
                    out_ref[m, 0:HROWS, 0, at] = tile
                else:
                    out_ref[m, HROWS:variables, 0, at] = tile[: variables - HROWS]


def strips(recv, variables):
    halves = recv.shape[0]
    full = pl.BlockSpec(memory_space=pltpu.VMEM)
    return pl.pallas_call(
        strips_kernel,
        in_specs=[full],
        out_specs=full,
        out_shape=jax.ShapeDtypeStruct((GROUP, variables, 1, halves * HALF), F32),
        compiler_params=SMALL,
        name="strips",
    )(recv)


def body(hidden_in, norm_gain, w_in, w_out, w_dec, observed, obs_count, obs_error):
    mem_dev, tok_dev, width = hidden_in.shape
    variables, lon_dev, lat_all = observed.shape
    n_mem, n_tile = lax.axis_size("mem"), lax.axis_size("tile")
    chips = n_tile // CORES
    mem, tile = lax.axis_index("mem"), lax.axis_index("tile")
    chip_place = lax.div(tile, CORES).astype(jnp.int32).reshape(1)
    place = lax.axis_index(("mem", "tile")).astype(jnp.int32).reshape(1)
    n_y = n_mem // 2
    by_chip = [
        [m * n_tile + c * CORES + k for m in range(n_mem) for k in range(CORES)] for c in range(chips)
    ]
    by_core = [[c * CORES + k for c in range(chips)] for k in range(CORES)]

    fields, *seen = forecast(
        place,
        n_y,
        hidden_in.reshape(mem_dev * tok_dev, width),
        norm_gain,
        w_in,
        w_out,
        w_dec,
        jnp.transpose(observed, (1, 2, 0)),
        jnp.transpose(obs_count, (1, 2, 0)),
    )
    halves = lax.all_to_all(
        fields, ("mem", "tile"), 0, 0, tiled=True, axis_index_groups=by_chip
    )

    mems, tiles = np.divmod(np.arange(n_mem * n_tile), n_tile)
    obs = []
    for k, move in enumerate(SENDS):
        targets = []
        for m, t in zip(mems.tolist(), tiles.tolist()):
            half, chip = served_here(m, t, move, (n_tile, n_y))
            targets.append((m * n_tile + t, half // CORES * n_tile + CORES * chip + half % CORES))
        obs.append(lax.ppermute(seen[k], ("mem", "tile"), targets))

    sums, weighted, mean, anomaly = pairs(halves, obs_error)
    smoothed = smooth(sums, weighted, mean, obs, chips)
    rows = lax.all_to_all(smoothed, "tile", 0, 0, tiled=True, axis_index_groups=by_core)
    increments = transform(chip_place, rows, anomaly)
    back = lax.all_to_all(
        increments, ("mem", "tile"), 0, 0, tiled=True, axis_index_groups=by_chip
    )
    return strips(back, variables)


def solution(mesh):
    return jax.shard_map(
        body,
        mesh=mesh,
        in_specs=(
            P("mem", "tile", None),
            P(),
            P(),
            P(),
            P(),
            P(None, "tile", None),
            P(None, "tile", None),
            P(),
        ),
        out_specs=P("mem", None, "tile", None),
        check_vma=False,
    )
```

```python
import functools
import math

import jax
import jax.numpy as jnp
import numpy as np
from jax import lax
from jax.experimental import pallas as pl
from jax.experimental.pallas import tpu as pltpu
from jax.sharding import PartitionSpec as P

RAD = 6
NS_ITERS = 4
F32 = jnp.float32
BF16 = jnp.bfloat16

LANES = 128
VROWS = 72
HROWS = 40
CORES = 2
HALF = 16
HALO = 8
WINDOW = HALF + 2 * HALO
POINTS = CORES * HALF
MEMBERS = 32
GROUP = 4
DIAGS = MEMBERS // 2 + 1
ROWS = DIAGS + 1
FF_BLOCK = 1024
TOKEN_BLOCK = 512

UNSEEN = 1e30
COUNT = 3.0

LARGE = pltpu.CompilerParams(vmem_limit_bytes=60 * 2**20)
SMALL = pltpu.CompilerParams(vmem_limit_bytes=12 * 2**20)


def lanes_of(shape):
    return lax.broadcasted_iota(jnp.int32, shape, len(shape) - 1)


def gelu(h):
    inner = h * (math.sqrt(2.0 / math.pi) + (0.044715 * math.sqrt(2.0 / math.pi)) * (h * h))
    half = 0.5 * h
    return half + half * jnp.tanh(inner)


SENDS = (0, -1)


def served(mem, tile, move, ways):
    n_tile, n_y = ways
    half = lax.rem(tile + (n_tile + move), n_tile)
    to_mem = lax.div(half, CORES)
    z_lo, y = lax.div(mem, n_y), lax.rem(mem, n_y)
    to_z_lo, to_y = lax.div(to_mem, n_y), lax.rem(to_mem, n_y)
    chip = lax.div(tile, CORES)
    x, z_hi = lax.div(chip, 2), lax.rem(chip, 2)
    n_x = n_tile // (2 * CORES)
    to_x = lax.rem(x + 2 + to_y - y + 2 * n_x, n_x)
    to_z_hi = lax.rem(z_hi + z_lo + to_z_lo, 2)
    return half, 2 * to_x + to_z_hi


def served_here(mem, tile, move, ways):
    n_tile, n_y = ways
    half = (tile + n_tile + move) % n_tile
    to_mem = half // CORES
    z_lo, y = mem // n_y, mem % n_y
    to_z_lo, to_y = to_mem // n_y, to_mem % n_y
    chip = tile // CORES
    x, z_hi = chip // 2, chip % 2
    n_x = n_tile // (2 * CORES)
    to_x = (x + 2 + to_y - y) % n_x
    to_z_hi = (z_hi + z_lo + to_z_lo) % 2
    return half, 2 * to_x + to_z_hi


def forecast_kernel(
    place_ref, x_ref, gain_ref, win_ref, wout_ref, wdec_ref, obs_ref, count_ref, out_ref, west_ref, east_ref,
    normed, acc, decoder, *, n_y,
):
    step = pl.program_id(0)
    steps = pl.num_programs(0)
    tokens = x_ref.shape[0]
    blocks = tokens // TOKEN_BLOCK
    lon_all = tokens // GROUP

    @pl.when(step == 0)
    def _():
        gain = gain_ref[...].astype(F32).reshape(1, -1)
        n_tile = out_ref.shape[0]
        mem, tile = lax.div(place_ref[0], n_tile), lax.rem(place_ref[0], n_tile)
        for seen_ref, move in zip((west_ref, east_ref), SENDS):
            _, chip = served(mem, tile, move, (n_tile, n_y))
            for r in range(CORES):
                row = CORES * chip + r
                seen_ref[r] = jnp.where(count_ref[:, row, :] > 0, obs_ref[:, row, :], UNSEEN)
        decoder[...] = jnp.zeros_like(decoder)
        decoder[0 : wdec_ref.shape[0], :] = wdec_ref[...].astype(F32)
        for r in range(tokens // 128):
            xf = x_ref[pl.ds(r * 128, 128), :].astype(F32)
            centred = xf - jnp.mean(xf, axis=-1, keepdims=True)
            spread = jnp.mean(centred * centred, axis=-1, keepdims=True)
            normed[pl.ds(r * 128, 128), :] = (centred * lax.rsqrt(spread + 1e-05) * gain).astype(BF16)

    def up(r):
        return jnp.dot(
            normed[pl.ds(r * TOKEN_BLOCK, TOKEN_BLOCK), :], win_ref[...], preferred_element_type=F32
        )

    def run(first):
        hidden = up(0)
        for r in range(blocks):
            following = up(r + 1) if r + 1 < blocks else None
            down = jnp.dot(gelu(hidden).astype(BF16), wout_ref[...], preferred_element_type=F32)
            at = pl.ds(r * TOKEN_BLOCK, TOKEN_BLOCK)
            if first:
                acc[at, :] = down
            else:
                acc[at, :] += down
            hidden = following

    @pl.when(step == 0)
    def _():
        run(True)

    @pl.when(step > 0)
    def _():
        run(False)

    @pl.when(step == steps - 1)
    def _():
        wdec = decoder[...].astype(BF16)
        contract = (((1,), (1,)), ((), ()))
        for r in range(blocks):
            at = pl.ds(r * TOKEN_BLOCK, TOKEN_BLOCK)
            layer_out = (x_ref[at, :].astype(F32) + acc[at, :]).astype(BF16)
            fields = lax.dot_general(layer_out, wdec, contract, preferred_element_type=F32)
            acc[at, 0 : 2 * HROWS] = fields
        for h in range(lon_all // HALF):
            window = []
            for m in range(GROUP):
                for at in (HALF * h, HALF * (h + 1)):
                    window.append(acc[pl.ds(m * lon_all + at % lon_all, HALF), 0:LANES])
            out_ref[h] = jnp.concatenate(window, axis=0).T[:VROWS].astype(BF16)


def forecast(place, n_y, x, gain, w_in, w_out, w_dec, observed, obs_count):
    tokens, width = x.shape
    hidden = w_in.shape[1]
    halves = tokens // GROUP // HALF
    lon_dev, _, variables = observed.shape
    whole = pl.BlockSpec(observed.shape, lambda s: (0, 0, 0))
    return pl.pallas_call(
        functools.partial(forecast_kernel, n_y=n_y),
        grid=(hidden // FF_BLOCK,),
        in_specs=[
            pl.BlockSpec(memory_space=pltpu.SMEM),
            pl.BlockSpec((tokens, width), lambda s: (0, 0)),
            pl.BlockSpec((width,), lambda s: (0,)),
            pl.BlockSpec((width, FF_BLOCK), lambda s: (0, s)),
            pl.BlockSpec((FF_BLOCK, width), lambda s: (s, 0)),
            pl.BlockSpec(w_dec.shape, lambda s: (0, 0)),
            whole,
            whole,
        ],
        out_specs=(
            pl.BlockSpec((halves, VROWS, LANES), lambda s: (0, 0, 0)),
            pl.BlockSpec((CORES, lon_dev, variables), lambda s: (0, 0, 0)),
            pl.BlockSpec((CORES, lon_dev, variables), lambda s: (0, 0, 0)),
        ),
        out_shape=(
            jax.ShapeDtypeStruct((halves, VROWS, LANES), BF16),
            jax.ShapeDtypeStruct((CORES, lon_dev, variables), F32),
            jax.ShapeDtypeStruct((CORES, lon_dev, variables), F32),
        ),
        scratch_shapes=[
            pltpu.VMEM((tokens, width), BF16),
            pltpu.VMEM((tokens, width), F32),
            pltpu.VMEM((2 * HROWS, width), F32),
        ],
        compiler_params=LARGE,
        cost_estimate=pl.CostEstimate(
            flops=4 * tokens * width * hidden, bytes_accessed=4 * width * hidden, transcendentals=0
        ),
        name="forecast",
    )(place, x, gain, w_in, w_out, w_dec, observed, obs_count)


def sum_over_groups(tile, width):
    while width < LANES:
        tile = tile + pltpu.roll(tile, width, 1)
        width *= 2
    return tile


def shifted_tile(tiles, index, shift, width):
    move = shift * width
    if not move:
        return tiles(index)
    here = pltpu.roll(tiles(index), LANES - move, 1)
    there = pltpu.roll(tiles(index + 1), LANES - move, 1)
    return jnp.where(lanes_of(here.shape) < LANES - move, here, there)


def pair_sums(fields, prec, width, weighted, moved, put):
    count = len(fields)
    per = LANES // width
    total = fields[0]
    for tile in fields[1:]:
        total = total + tile
    mean = sum_over_groups(total, width) / MEMBERS
    anomalies = []
    for k in range(count):
        anomaly = fields[k] - mean
        anomalies.append(anomaly)
        weighted[k] = (anomaly * prec).astype(BF16).astype(F32)
        moved[0, k] = anomaly.astype(BF16).astype(F32)
    for t in range(1, per):
        for k in range(count):
            moved[t, k] = shifted_tile(lambda j: moved[0, j % count], k, t, width)
    for s in range(DIAGS):
        on, t = divmod(s, per)
        for k in range(count):
            put(s, k, jnp.sum(weighted[k] * moved[t, (k + on) % count], axis=0, keepdims=True))
    return mean, anomalies


def pairs_kernel(recv_ref, err_ref, sums, weighted, mean_ref, anom_ref, wide, moved):
    tiles = recv_ref.shape[0] // CORES
    variables = err_ref.shape[0]
    wide[...] = jnp.zeros_like(wide)
    wide[0:1, 0:variables] = err_ref[...].reshape(1, variables)
    err = jnp.broadcast_to(wide[0:1, :], (LANES, LANES)).T[:VROWS]
    is_variable = lax.broadcasted_iota(jnp.int32, err.shape, 0) < variables
    prec = jnp.where(is_variable, COUNT / (err * err), 0.0)

    sums[pl.ds(DIAGS * tiles, tiles), :] = jnp.zeros((tiles, CORES * LANES), F32)
    anomalies = []
    for r in range(CORES):

        def put(s, k, row):
            sums[pl.ds(s * tiles + k, 1), r * LANES : (r + 1) * LANES] = row

        fields = [recv_ref[CORES * m + r].astype(F32) for m in range(tiles)]
        mean, anomaly = pair_sums(fields, prec, WINDOW, weighted.at[r], moved.at[r], put)
        mean_ref[r] = mean
        anomalies.append(anomaly)
    lower = lanes_of((VROWS, LANES)) % POINTS < HALF
    for k in range(tiles):
        anom_ref[k] = jnp.where(
            lower,
            pltpu.roll(anomalies[0][k], LANES - HALO, 1),
            pltpu.roll(anomalies[1][k], HALF - HALO, 1),
        )


def two_parts(x):
    high = x.astype(BF16)
    return high, (x - high.astype(F32)).astype(BF16)


def smooth_kernel(sums_ref, weighted, mean_ref, west_ref, east_ref, taper_ref, out_ref, wide, sums):
    tiles = weighted.shape[1]
    variables = west_ref.shape[2]
    wide[...] = jnp.zeros_like(wide)
    for r in range(CORES):
        at = slice(r * LANES, (r + 1) * LANES)
        wide[0:HALF, 0:variables] = west_ref[r]
        wide[HALF:WINDOW, 0:variables] = east_ref[r]
        obs = jnp.concatenate([wide[...]] * GROUP, axis=0).T[:VROWS]
        is_seen = obs[0:1] < 0.5 * UNSEEN
        innovation = obs - mean_ref[r]
        diags = sums_ref[0 : DIAGS * tiles, at]
        sums[0 : DIAGS * tiles, at] = jnp.where(is_seen, diags, 0.0)
        for k in range(tiles):
            row = jnp.sum(weighted[r, k] * innovation, axis=0, keepdims=True)
            sums[pl.ds(DIAGS * tiles + k, 1), at] = jnp.where(is_seen, row, 0.0)
    high, low = two_parts(sums[...])
    taper_high, taper_low = two_parts(taper_ref[...])
    smooth = jnp.dot(high, taper_low, preferred_element_type=F32)
    smooth = smooth + jnp.dot(low, taper_high, preferred_element_type=F32)
    smooth = (smooth + jnp.dot(high, taper_high, preferred_element_type=F32)).astype(BF16)
    for c in range(out_ref.shape[0]):
        out_ref[c] = smooth


def taper_of(offset):
    offset = np.asarray(offset, np.float32)
    ratio = offset / np.float32(RAD + 1.0)
    return np.where(np.abs(offset) <= RAD, (1.0 - ratio * ratio) ** 2, 0.0).astype(np.float32)


def longitude_taper():
    lat, rest = np.divmod(np.arange(CORES * LANES), LANES)
    member, col = np.divmod(rest, WINDOW)
    out_member, rest = np.divmod(np.arange(LANES), POINTS)
    out_lat, out_col = np.divmod(rest, HALF)
    same = (lat[:, None] == out_lat[None, :]) & (member[:, None] == out_member[None, :])
    weight = taper_of(col[:, None] - HALO - out_col[None, :])
    return jnp.asarray(np.where(same, weight, 0.0).astype(np.float32))


def pairs(recv, err):
    tiles = recv.shape[0] // CORES
    full = pl.BlockSpec(memory_space=pltpu.VMEM)
    return pl.pallas_call(
        pairs_kernel,
        in_specs=[full] * 2,
        out_specs=(full,) * 4,
        out_shape=(
            jax.ShapeDtypeStruct((ROWS * tiles, CORES * LANES), F32),
            jax.ShapeDtypeStruct((CORES, tiles, VROWS, LANES), F32),
            jax.ShapeDtypeStruct((CORES, VROWS, LANES), F32),
            jax.ShapeDtypeStruct((tiles, VROWS, LANES), F32),
        ),
        scratch_shapes=[
            pltpu.VMEM((8, LANES), F32),
            pltpu.VMEM((CORES, LANES // WINDOW, tiles, VROWS, LANES), F32),
        ],
        compiler_params=SMALL,
        name="pairs",
    )(recv, err)


def smooth(sums, weighted, mean, obs, chips):
    full = pl.BlockSpec(memory_space=pltpu.VMEM)
    return pl.pallas_call(
        smooth_kernel,
        in_specs=[full] * 6,
        out_specs=full,
        out_shape=jax.ShapeDtypeStruct((chips, sums.shape[0], LANES), BF16),
        scratch_shapes=[pltpu.VMEM((WINDOW, LANES), F32), pltpu.VMEM(sums.shape, F32)],
        compiler_params=SMALL,
        name="smooth",
    )(sums, weighted, mean, *obs, longitude_taper())


def on_by(x, n):
    sub, t = divmod(n % MEMBERS, GROUP)
    if t:
        move = LANES - POINTS * t
        x = pltpu.roll(x, move, 1)
        x = jnp.where(lanes_of(x.shape) < move, x, pltpu.roll(x, 7, 0))
    if sub:
        x = pltpu.roll(x, 8 - sub, 0)
    return x


def shifted_sum(term):
    total = None
    for t in range(GROUP - 1, -1, -1):
        inner = None
        for a in range(MEMBERS // GROUP - 1, -1, -1):
            part = term(GROUP * a + t)
            inner = part if inner is None else on_by(inner, GROUP) + part
        total = inner if total is None else on_by(total, 1) + inner
    return total


def spread(right, turned):
    for u in range(MEMBERS):
        value = right[u]
        for a in range(MEMBERS // GROUP):
            turned[a, u] = on_by(value, GROUP * a)


def product(left, turned, out, scale=None, shift=None):
    moved = [on_by(left[(-t) % MEMBERS], t // GROUP * GROUP) for t in range(MEMBERS)]
    for s in range(DIAGS):
        value = None
        for t in range(GROUP - 1, -1, -1):
            parts = [
                moved[at] * turned[at // GROUP, (s - at) % MEMBERS] for at in range(t, MEMBERS, GROUP)
            ]
            while len(parts) > 1:
                parts = [a + b for a, b in zip(parts[::2], parts[1::2])]
            value = parts[0] if value is None else on_by(value, 1) + parts[0]
        if scale is not None:
            value = scale * value
            if s == 0:
                value = value + shift
        out[s] = value
    mirror(out)


def mirror(out):
    for s in range(1, MEMBERS - DIAGS + 1):
        out[MEMBERS - s] = on_by(out[s], -s)


def latitude_weight(offset):
    ratio = offset.astype(F32) * (1.0 / (RAD + 1.0))
    return jnp.where(jnp.abs(offset) <= RAD, (1.0 - ratio * ratio) * (1.0 - ratio * ratio), 0.0)


def transform_kernel(place_ref, recv_ref, anom_ref, out_ref, bank, turned, moved, coeff):
    chips = recv_ref.shape[0]
    tiles = anom_ref.shape[0]
    same, south, north = None, None, None
    for c in range(chips):
        sums = recv_ref[c].astype(F32)
        offset = CORES * (place_ref[0] - c)
        parts = [latitude_weight(offset + d) * sums for d in (0, -1, 1)]
        if c == 0:
            same, south, north = parts
        else:
            same, south, north = same + parts[0], south + parts[1], north + parts[2]
    lower = lanes_of(same.shape) % POINTS < HALF
    local = same + jnp.where(
        lower, pltpu.roll(south, LANES - HALF, 1), pltpu.roll(north, HALF, 1)
    )
    diag = [local[s * tiles : (s + 1) * tiles] for s in range(ROWS)]
    innov = diag[DIAGS]
    diag[0] = diag[0] + (MEMBERS - 1.0)
    gram, root, inv_root, corr = bank.at[0], bank.at[1], bank.at[2], bank.at[3]
    other_root, other_inv = bank.at[4], bank.at[5]
    square = None
    for s in range(DIAGS):
        part = diag[s] * diag[s]
        if 0 < s < DIAGS - 1:
            part = part + part
        square = part if square is None else square + part
    square = jnp.broadcast_to(jnp.sum(square, axis=0, keepdims=True), square.shape)
    frob = jnp.sqrt(sum_over_groups(square, POINTS))
    inv_frob = 1.0 / frob
    for s in range(DIAGS):
        gram[s] = diag[s] * inv_frob
    mirror(gram)
    for s in range(MEMBERS):
        inv_root[s] = -0.5 * gram[s] + (1.5 if s == 0 else 0.0)
    spread(inv_root, turned)
    product(gram, turned, root)
    for sweep in range(1, NS_ITERS):
        spread(root, turned)
        product(inv_root, turned, corr, -0.5, 1.5)
        spread(corr, turned)
        if sweep < NS_ITERS - 1:
            product(root, turned, other_root)
        product(inv_root, turned, other_inv)
        root, other_root = other_root, root
        inv_root, other_inv = other_inv, inv_root
    half = shifted_sum(lambda t: inv_root[(-t) % MEMBERS] * innov)
    mean_weights = shifted_sum(lambda t: inv_root[(-t) % MEMBERS] * half) * inv_frob
    factor = math.sqrt(MEMBERS - 1.0) / jnp.sqrt(frob)
    for s in range(MEMBERS):
        value = inv_root[s] * factor + on_by(mean_weights, s)
        coeff[pl.ds(s * tiles, tiles), :] = value.astype(BF16).astype(F32)
    for k in range(tiles):
        moved[0, k] = anom_ref[k].astype(BF16).astype(F32)
    for t in range(1, GROUP):
        for k in range(tiles):
            moved[t, k] = shifted_tile(lambda j: moved[0, j % tiles], k, t, POINTS)
    for k in range(tiles):
        mixed = -anom_ref[k]
        for on in range(tiles):
            parts = [
                moved[t, (k + on) % tiles] * coeff[pl.ds((GROUP * on + t) * tiles + k, 1), :]
                for t in range(GROUP)
            ]
            mixed = mixed + ((parts[0] + parts[1]) + (parts[2] + parts[3]))
        low = mixed[:HROWS]
        high = jnp.concatenate([mixed[HROWS:], jnp.zeros((2 * HROWS - VROWS, LANES), F32)], axis=0)
        first = lanes_of(low.shape) % POINTS < HALF
        out_ref[CORES * k] = jnp.where(first, low, pltpu.roll(high, HALF, 1)).astype(BF16)
        out_ref[CORES * k + 1] = jnp.where(first, pltpu.roll(low, LANES - HALF, 1), high).astype(BF16)


def transform(place, recv, anomaly):
    tiles = anomaly.shape[0]
    full = pl.BlockSpec(memory_space=pltpu.VMEM)
    return pl.pallas_call(
        transform_kernel,
        in_specs=[pl.BlockSpec(memory_space=pltpu.SMEM), full, full],
        out_specs=full,
        out_shape=jax.ShapeDtypeStruct((CORES * tiles, HROWS, LANES), BF16),
        scratch_shapes=[
            pltpu.VMEM((6, MEMBERS, tiles, LANES), F32),
            pltpu.VMEM((MEMBERS // GROUP, MEMBERS, tiles, LANES), F32),
            pltpu.VMEM((GROUP, tiles, VROWS, LANES), F32),
            pltpu.VMEM((MEMBERS * tiles, LANES), F32),
        ],
        compiler_params=SMALL,
        name="transform",
    )(place, recv, anomaly)


def strips_kernel(recv_ref, out_ref):
    halves = recv_ref.shape[0]
    variables = out_ref.shape[1]
    per = LANES // HALF
    parts = [recv_ref[h].astype(F32) for h in range(halves)]
    group = lax.rem(lanes_of(parts[0].shape) + (LANES - HALO), LANES) // HALF
    first = lanes_of(parts[0].shape) < HALO
    held = lanes_of(parts[0].shape) // HALF
    moved = []
    for c in range(halves // per):
        for way in range(per):
            tile = parts[per * c + way]
            for g in range(1, per):
                tile = jnp.where(held == g, parts[per * c + (way + g) % per], tile)
            moved.append(pltpu.roll(tile, (HALF * way + HALO) % LANES, 1))
    for m in range(GROUP):
        for side in range(2):
            tiles = []
            for c in range(halves // per):
                tile = None
                for j in range(per):
                    piece = moved[per * c + (j - 2 * m - side) % per]
                    tile = piece if tile is None else jnp.where(group == j, piece, tile)
                tiles.append(tile)
            for c in range(len(tiles)):
                tile = jnp.where(first, tiles[c - 1], tiles[c])
                at = pl.ds(c * LANES, LANES)
                if side == 0:
                    out_ref[m, 0:HROWS, 0, at] = tile
                else:
                    out_ref[m, HROWS:variables, 0, at] = tile[: variables - HROWS]


def strips(recv, variables):
    halves = recv.shape[0]
    full = pl.BlockSpec(memory_space=pltpu.VMEM)
    return pl.pallas_call(
        strips_kernel,
        in_specs=[full],
        out_specs=full,
        out_shape=jax.ShapeDtypeStruct((GROUP, variables, 1, halves * HALF), F32),
        compiler_params=SMALL,
        name="strips",
    )(recv)


def body(hidden_in, norm_gain, w_in, w_out, w_dec, observed, obs_count, obs_error):
    mem_dev, tok_dev, width = hidden_in.shape
    variables, lon_dev, lat_all = observed.shape
    n_mem, n_tile = lax.axis_size("mem"), lax.axis_size("tile")
    chips = n_tile // CORES
    mem, tile = lax.axis_index("mem"), lax.axis_index("tile")
    chip_place = lax.div(tile, CORES).astype(jnp.int32).reshape(1)
    place = lax.axis_index(("mem", "tile")).astype(jnp.int32).reshape(1)
    n_y = n_mem // 2
    by_chip = [
        [m * n_tile + c * CORES + k for m in range(n_mem) for k in range(CORES)] for c in range(chips)
    ]
    by_core = [[c * CORES + k for c in range(chips)] for k in range(CORES)]

    fields, *seen = forecast(
        place,
        n_y,
        hidden_in.reshape(mem_dev * tok_dev, width),
        norm_gain,
        w_in,
        w_out,
        w_dec,
        jnp.transpose(observed, (1, 2, 0)),
        jnp.transpose(obs_count, (1, 2, 0)),
    )
    halves = lax.all_to_all(
        fields, ("mem", "tile"), 0, 0, tiled=True, axis_index_groups=by_chip
    )

    mems, tiles = np.divmod(np.arange(n_mem * n_tile), n_tile)
    obs = []
    for k, move in enumerate(SENDS):
        targets = []
        for m, t in zip(mems.tolist(), tiles.tolist()):
            half, chip = served_here(m, t, move, (n_tile, n_y))
            targets.append((m * n_tile + t, half // CORES * n_tile + CORES * chip + half % CORES))
        obs.append(lax.ppermute(seen[k], ("mem", "tile"), targets))

    sums, weighted, mean, anomaly = pairs(halves, obs_error)
    smoothed = smooth(sums, weighted, mean, obs, chips)
    rows = lax.all_to_all(smoothed, "tile", 0, 0, tiled=True, axis_index_groups=by_core)
    increments = transform(chip_place, rows, anomaly)
    back = lax.all_to_all(
        increments, ("mem", "tile"), 0, 0, tiled=True, axis_index_groups=by_chip
    )
    return strips(back, variables)


def solution(mesh):
    return jax.shard_map(
        body,
        mesh=mesh,
        in_specs=(
            P("mem", "tile", None),
            P(),
            P(),
            P(),
            P(),
            P(None, "tile", None),
            P(None, "tile", None),
            P(),
        ),
        out_specs=P("mem", None, "tile", None),
        check_vma=False,
    )
```
